32 devices in a mesh: modes: 16 (over z, y, core), dom: 2 (over x).
Axes of the slice: x: 2, y: 2, z: 4, core: 2. Of those that a mesh axis runs over, the one named last changes fastest.
Arguments:
- velocity: float32 [3, 256, 81, 256], P(None, 'modes', None, 'dom'), may hold values from -6 to 6
- slot_of_cell: int32 [2, 128], P('dom'), may hold values from 0 to 127, each once within a row
- elem_mats: float32 [4, 81, 81], replicated, may hold values from -0.625 to 0.625
- geometry: float32 [4, 256], P(None, 'dom'), may hold values from 0.5 to 2
Outputs:
- result: float32 [3, 256, 81, 256], P(None, 'modes', None, 'dom')
The draws below stay inside these ranges and needn't reach their ends.
Inputs may be any that keep to these rules, and one draw needn't show every extreme that they name: `slot_of_cell`: each row is a permutation of the slots 0 to 127.
All inputs are finite; a program needn't handle non-finite values.
Results may differ from the reference program's by a relative error of at most 0.0003.
Values sent between devices are 32-bit elements; how exact they have to be, the bound alone decides.
No kernel may reach another device: no remote copies, remote signals or barrier semaphores. Data moves between devices by JAX's collectives and lax.ppermute only.
A program may use at most 128 MiB of HBM per device.

```python
import math
import jax
import jax.numpy as jnp
from jax import lax

EX = 16
EY = 8
ELEMS_DEV = 128
PARTS_SIZE = 2
ELEMS = 256
PLANES = 256


def shard_levels(key, extent, split, least, largest):
    level = 1.0
    for position, blocks in split:
        draws = jax.random.uniform(jax.random.fold_in(jax.random.fold_in(key, 6), position), (blocks,), jnp.float32, least / len(split), largest / len(split))
        level = level * jnp.repeat(jnp.exp(draws), extent[position] // blocks).reshape((-1,) + (1,) * (len(extent) - 1 - position))
    return level


def bell_draw(own_key, extent, spread, most, shards=(), kind=jnp.bfloat16):
    gain = shard_levels(own_key, extent, shards, -0.22, 0.18) if shards else 1.0
    result = jax.random.normal(own_key, extent, jnp.float32) * spread * gain
    return jnp.minimum(jnp.maximum(result, -most), most).astype(kind)


def setup_inputs(seed: int = 0) -> dict:
    arg_keys = jax.random.split(jax.random.key(seed), 5)
    velocity = bell_draw(arg_keys[0], (3, PLANES, 81, ELEMS), 1.0, 6.0, ((1, 16), (3, 2)), jnp.float32)
    slot_of_cell = jax.vmap(lambda own: jax.random.permutation(own, ELEMS_DEV))(jax.random.split(arg_keys[1], PARTS_SIZE)).reshape((PARTS_SIZE, ELEMS_DEV)).astype(jnp.int32)
    elem_mats = bell_draw(arg_keys[2], (4, 81, 81), 81 ** -0.5, 0.625, (), jnp.float32)
    geometry = jnp.clip(jnp.exp(math.log(2.0) - 1.3862944 * jax.random.uniform(arg_keys[3], (4, ELEMS), jnp.float32) ** shard_levels(arg_keys[3], (4, ELEMS), ((1, 2),), -0.2, 0.2)), 0.5, 2.0)
    return dict(velocity=velocity, slot_of_cell=slot_of_cell, elem_mats=elem_mats, geometry=geometry)


def tables(length):
    indices = jnp.arange(length, dtype=jnp.int32)
    halfway = length // 2
    wavenum = jnp.where(indices <= halfway, indices, indices - halfway)
    phases = (wavenum[:, None] * indices[None, :]) % length
    angles = phases.astype(jnp.float32) * jnp.float32(2.0 * math.pi / length)
    forward = jnp.where((indices <= halfway)[:, None], jnp.cos(angles), jnp.sin(angles))
    weights = jnp.where((indices == 0) | (indices == halfway), jnp.float32(1.0 / length), jnp.float32(2.0 / length))
    inverse = (forward * weights[:, None]).T
    helm_shift = 1.0 + (8.0 * wavenum.astype(jnp.float32) / length) ** 2
    return forward, inverse, helm_shift


def invert(order):
    return jnp.zeros_like(order).at[order].set(jnp.arange(order.shape[0], dtype=jnp.int32))


def assemble(values, slot_of_cell):
    planes = values.shape[0]
    parts = slot_of_cell.shape[0]
    per_part = slot_of_cell.shape[1]
    shaped = values.reshape(planes, 81, parts, per_part)
    picked = jnp.take_along_axis(shaped, slot_of_cell[None, None], axis=3)
    cells_grid = picked.reshape(planes, 9, 9, parts * EX, EY)
    along = cells_grid[:, 8] + jnp.roll(cells_grid[:, 0], -1, axis=2)
    cells_grid = cells_grid.at[:, 8].set(along).at[:, 0].set(jnp.roll(along, 1, axis=2))
    across = cells_grid[:, :, 8, :, :-1] + cells_grid[:, :, 0, :, 1:]
    cells_grid = cells_grid.at[:, :, 8, :, :-1].set(across).at[:, :, 0, :, 1:].set(across)
    flat = cells_grid.reshape(planes, 81, parts, per_part)
    inverse_slot = jax.vmap(invert)(slot_of_cell)
    restored = jnp.take_along_axis(flat, inverse_slot[None, None], axis=3)
    return restored.reshape(planes, 81, parts * per_part)


def reference(velocity, slot_of_cell, elem_mats, geometry):
    forward, inverse, helm_shift = tables(PLANES)

    def component(index):
        product = velocity[index] * velocity[(index + 1) % 3]
        spectra = jnp.einsum('mp,pne->mne', forward, product, precision=lax.Precision.HIGHEST)
        images = jnp.einsum('tij,mje->tmie', elem_mats, spectra, precision=lax.Precision.HIGHEST)
        stiff = images[0] * geometry[0] + images[1] * geometry[1] + images[2] * geometry[2]
        applied = stiff + helm_shift[:, None, None] * (images[3] * geometry[3])
        summed = assemble(applied, slot_of_cell)
        return jnp.einsum('pm,mne->pne', inverse, summed, precision=lax.Precision.HIGHEST)

    return lax.map(component, jnp.arange(3, dtype=jnp.int32))
```

```python
import functools

import jax
import jax.numpy as jnp
import numpy as np
from jax import lax
from jax.experimental import pallas as pl
from jax.experimental.pallas import tpu as pltpu
from jax.sharding import PartitionSpec as P

EX = 16
EY = 8
NODES = 81
INNER = 64
ROWS = INNER + 3
ACROSS, RIGHT, LEFT = INNER, INNER + 1, INNER + 2
VMEM = 48 * 1024 * 1024

f32 = jnp.float32
bf16 = jnp.bfloat16


def split(values):
    high = values.astype(bf16)
    return high, (values - high.astype(f32)).astype(bf16)


def operator(length):
    half = length // 2
    waves = np.arange(half + 1)
    weights = np.where((waves == 0) | (waves == half), 1.0, 2.0) / length
    sigma = 1.0 + (8.0 * waves / length) ** 2
    distance = np.arange(length)
    phases = (distance[:, None] * waves[None, :]) % length
    row = (np.cos(phases * (2.0 * np.pi / length)) * (weights * sigma)).sum(1)
    full = row[(distance[:, None] - distance[None, :]) % length].astype(np.float32)
    high = full.astype(jnp.bfloat16)
    low = (full - high.astype(np.float32)).astype(jnp.bfloat16)
    return high, low


def selector(slots):
    slot = lax.broadcasted_iota(jnp.int32, (EX * EY, EX * EY), 0)
    return jnp.where(slot == slots, 1.0, 0.0).astype(f32)


def lane_index(shape):
    return lax.broadcasted_iota(jnp.int32, shape, len(shape) - 1)


def element_kernel(terms, vel_ref, slots_ref, mats_ref, geo_ref, out_ref, left_ref, nodes_ref):
    depth = vel_ref.shape[1]
    count = len(terms)
    select = selector(slots_ref[...])
    geo = jnp.dot(geo_ref[...], select, precision=lax.Precision.HIGHEST, preferred_element_type=f32)
    select = select.astype(bf16)
    left_ref[...] = jnp.zeros_like(left_ref)
    for place, term in enumerate(terms):
        high, low = split(mats_ref[term])
        left_ref[place, :NODES, 0:NODES] = high
        left_ref[place, :NODES, 128 : 128 + NODES] = high
        left_ref[place, :NODES, 256 : 256 + NODES] = low
    left = left_ref[...].reshape(count * 96, 384)
    lane = lane_index((depth, EX * EY))
    across = lane % EY
    pad_rows = jnp.zeros((96 - NODES, EX * EY), f32)
    pad_deep = jnp.zeros((32, 2 * EX * EY), bf16)
    for c in range(3):
        for pair in range(depth // 2):
            parts = []
            for p in (2 * pair, 2 * pair + 1):
                product = vel_ref[c, p] * vel_ref[(c + 1) % 3, p]
                high, low = split(jnp.concatenate([product, pad_rows], axis=0))
                cells = jnp.dot(
                    jnp.concatenate([high, low], axis=0), select, preferred_element_type=f32
                )
                parts.append(cells.astype(bf16))
            both = jnp.concatenate(parts, axis=1)
            high = jnp.concatenate([both[:96], pad_deep], axis=0)
            low = jnp.concatenate([both[96:], pad_deep], axis=0)
            right = jnp.concatenate([high, low, high], axis=0)
            images = jnp.dot(left, right, preferred_element_type=f32)
            for place, p in enumerate((2 * pair, 2 * pair + 1)):
                total = 0.0
                for t, term in enumerate(terms):
                    total = total + (
                        images[96 * t : 96 * t + 88, 128 * place : 128 * place + 128]
                        * geo[term : term + 1]
                    )
                nodes_ref[c, pl.ds(p, 88, stride=depth), :] = total
        node = lambda i, j: nodes_ref[c, (9 * i + j) * depth : (9 * i + j + 1) * depth, :]

        def first(j):
            return node(0, j) + jnp.where(lane >= EY, pltpu.roll(node(8, j), EY, 1), 0.0)

        def store(row, value):
            out_ref[c * ROWS + row] = value

        def join(low, high):
            return low + jnp.where(across > 0, pltpu.roll(high, 1, 1), 0.0)

        end = jnp.zeros((depth, EX * EY), f32)
        for i in range(8):
            column = [first(j) if i == 0 else node(i, j) for j in range(9)]
            store(8 * i, join(column[0], column[8]))
            for j in range(1, 8):
                store(8 * i + j, column[j])
            shift = (i + 1 - EY) % (EX * EY)
            ended = column[8] if shift == 0 else pltpu.roll(column[8], shift, 1)
            end = jnp.where(across == i, ended, end)
        store(ACROSS, end)
        for row, i, origin in ((RIGHT, 8, (EX - 1) * EY), (LEFT, 0, 0)):
            last = node(i, 8)
            face = jnp.where(lane == INNER, pltpu.roll(last, (INNER - origin - EY + 1) % (EX * EY), 1), 0.0)
            for j in range(8):
                value = join(node(i, 0), last) if j == 0 else node(i, j)
                shift = (8 * j - origin) % (EX * EY)
                moved = value if shift == 0 else pltpu.roll(value, shift, 1)
                face = jnp.where(lane // EY == j, moved, face)
            store(row, face)


def elements(terms, velocity, slot_of_cell, elem_mats, geometry, rows):
    depth = velocity.shape[1]
    step = 8
    lanes = EX * EY
    return pl.pallas_call(
        functools.partial(element_kernel, terms),
        grid=(depth // step,),
        in_specs=[
            pl.BlockSpec((3, step, NODES, lanes), lambda k: (0, k, 0, 0)),
            pl.BlockSpec((1, lanes), lambda k: (0, 0)),
            pl.BlockSpec((4, NODES, NODES), lambda k: (0, 0, 0)),
            pl.BlockSpec((4, lanes), lambda k: (0, 0)),
        ],
        out_specs=pl.BlockSpec((rows, step, lanes), lambda k: (0, k, 0)),
        out_shape=jax.ShapeDtypeStruct((rows, depth, lanes), f32),
        scratch_shapes=[
            pltpu.VMEM((len(terms), 96, 384), bf16),
            pltpu.VMEM((3, 88 * step, lanes), f32),
        ],
        compiler_params=pltpu.CompilerParams(vmem_limit_bytes=VMEM),
        cost_estimate=pl.CostEstimate(
            flops=2 * 3 * depth * len(terms) * 96 * 384 * 128,
            bytes_accessed=4 * 3 * depth * 128 * (88 + 67),
            transcendentals=0,
        ),
        name="element_terms" if len(terms) > 1 else "element_mass",
    )(velocity, slot_of_cell, elem_mats, geometry)


def spanwise_kernel(x_ref, high_ref, low_ref, y_ref):
    parts, rows, depth, lanes = x_ref.shape
    length = parts * depth
    high, low = high_ref[...], low_ref[...]
    for r in range(0, rows, 2):
        width = min(2, rows - r)
        x = [x_ref[:, r + k].reshape(length, lanes) for k in range(width)]
        x = x[0] if width == 1 else jnp.concatenate(x, axis=1)
        x_high, x_low = split(x)
        y = jnp.dot(high, x_high, preferred_element_type=f32)
        y += jnp.dot(low, x_high, preferred_element_type=f32)
        y += jnp.dot(high, x_low, preferred_element_type=f32)
        for k in range(width):
            y_ref[:, r + k] = y[:, lanes * k : lanes * k + lanes].reshape(parts, depth, lanes)


def spanwise(values):
    parts, rows, depth, lanes = values.shape
    length = parts * depth
    high, low = operator(length)
    return pl.pallas_call(
        spanwise_kernel,
        out_shape=jax.ShapeDtypeStruct(values.shape, f32),
        compiler_params=pltpu.CompilerParams(vmem_limit_bytes=VMEM),
        cost_estimate=pl.CostEstimate(
            flops=6 * length * length * rows * lanes,
            bytes_accessed=8 * length * rows * lanes,
            transcendentals=0,
        ),
        name="spanwise",
    )(values, high, low)


def expand_kernel(u_ref, y_ref, faces_ref, slots_ref, out_ref, nodes_ref):
    depth, lanes = u_ref.shape[1:]
    select = selector(slots_ref[...]).astype(bf16)
    select = jnp.concatenate([select, select], axis=1)
    lane = lane_index((depth, lanes))
    across = lane % EY
    row = lambda q: u_ref[q] + y_ref[q]
    before, after = faces_ref[0, 0], faces_ref[1, 0]

    def put(i, j, value):
        high, low = split(value)
        nodes_ref[pl.ds((9 * i + j) * depth, depth), :] = jnp.concatenate([high, low], axis=1)

    end = row(ACROSS) + jnp.where(lane == 0, pltpu.roll(before, lanes - INNER, 1), 0.0)
    face = row(RIGHT) + after
    for i in range(8):
        for j in range(8):
            value = row(8 * i + j)
            if i == 0:
                moved = before if j == 0 else pltpu.roll(before, lanes - 8 * j, 1)
                value = value + jnp.where(lane < EY, moved, 0.0)
                moved = pltpu.roll(face, (lanes - EY - 8 * j) % lanes, 1) if j < 15 else face
                beyond = jnp.where(lane >= lanes - EY, moved, pltpu.roll(value, lanes - EY, 1))
                put(8, j, beyond)
                if j == 0:
                    corner = pltpu.roll(beyond, lanes - 1, 1)
            put(i, j, value)
            if j == 0:
                moved = end if i == 7 else pltpu.roll(end, EY - 1 - i, 1)
                last = jnp.where(across == EY - 1, moved, pltpu.roll(value, lanes - 1, 1))
                put(i, 8, last)
    corner = jnp.where(across == EY - 1, pltpu.roll(end, lanes - 1, 1), corner)
    corner = jnp.where(lane == lanes - 1, pltpu.roll(face, lanes - 1 - INNER, 1), corner)
    put(8, 8, corner)
    slots = lax.dot_general(
        nodes_ref[...], select, (((1,), (1,)), ((), ())), preferred_element_type=f32
    )
    result_ref = out_ref
    slots = slots.reshape(NODES, depth, lanes)
    for p in range(depth):
        result_ref[0, p] = slots[:, p, :]


def expand(u, y, faces, slot_of_cell):
    depth, lanes = u.shape[1:]
    return pl.pallas_call(
        expand_kernel,
        grid=(3,),
        in_specs=[
            pl.BlockSpec((ROWS, depth, lanes), lambda c: (c, 0, 0)),
            pl.BlockSpec((ROWS, depth, lanes), lambda c: (c, 0, 0)),
            pl.BlockSpec((2, 1, depth, lanes), lambda c: (0, c, 0, 0)),
            pl.BlockSpec((1, lanes), lambda c: (0, 0)),
        ],
        out_specs=pl.BlockSpec((1, depth, NODES, lanes), lambda c: (c, 0, 0, 0)),
        out_shape=jax.ShapeDtypeStruct((3, depth, NODES, lanes), f32),
        scratch_shapes=[pltpu.VMEM((NODES * depth, 2 * lanes), bf16)],
        compiler_params=pltpu.CompilerParams(vmem_limit_bytes=VMEM),
        cost_estimate=pl.CostEstimate(
            flops=2 * 3 * NODES * depth * 256 * 128,
            bytes_accessed=4 * 3 * depth * lanes * 222,
            transcendentals=0,
        ),
        name="expand",
    )(u, y, faces, slot_of_cell)


def swap(values):
    return lax.all_to_all(values, "modes", split_axis=0, concat_axis=0, tiled=True)


def local(velocity, slot_of_cell, elem_mats, geometry):
    depth = velocity.shape[1]
    lanes = velocity.shape[3]
    parts = lax.axis_size("modes")
    share = -(-3 * ROWS // parts)
    rows = share * parts
    z = elements((3,), velocity, slot_of_cell, elem_mats, geometry, rows)
    pencil = swap(z.reshape(parts, share * depth, lanes))
    u = elements((0, 1, 2), velocity, slot_of_cell, elem_mats, geometry, rows)
    y = spanwise(pencil.reshape(parts, share, depth, lanes))
    y = swap(y.reshape(parts, share * depth, lanes)).reshape(rows, depth, lanes)
    count = lax.axis_size("dom")
    forward = [(k, (k + 1) % count) for k in range(count)]
    backward = [(k, (k - 1) % count) for k in range(count)]

    def face(row):
        pick = lambda a: a[: 3 * ROWS].reshape(3, ROWS, depth, lanes)[:, row]
        return pick(u) + pick(y)

    before = lax.ppermute(face(RIGHT), "dom", forward)
    after = lax.ppermute(face(LEFT), "dom", backward)
    return expand(u, y, jnp.stack([before, after]), slot_of_cell)


def solution(mesh):
    in_specs = (P(None, "modes", None, "dom"), P("dom", None), P(), P(None, "dom"))
    out_specs = P(None, "modes", None, "dom")
    return jax.shard_map(local, mesh=mesh, in_specs=in_specs, out_specs=out_specs, check_vma=False)
```

```python
import functools
import math

import jax
import jax.numpy as jnp
import numpy as np
from jax import lax
from jax.experimental import pallas as pl
from jax.experimental.pallas import tpu as pltpu
from jax.sharding import PartitionSpec as P

EX = 16
EY = 8
LANES = EX * EY
NODES = 81
SIDE = 8
INNER = SIDE * (SIDE - 1)
FACE = SIDE * EY
ACROSS, RIGHT, LEFT, EXTRA = SIDE, SIDE + 1, SIDE + 2, SIDE + 3
DEEP = 96
VMEM = 48 * 1024 * 1024
WIDE = 60 * 1024 * 1024

f32 = jnp.float32
bf16 = jnp.bfloat16


def split(values):
    high = values.astype(bf16)
    return high, (values - high.astype(f32)).astype(bf16)


class Layout:

    def __init__(self, parts):
        self.outer = max(d for d in range(1, math.isqrt(parts) + 1) if parts % d == 0)
        self.inner = parts // self.outer
        assert self.inner & (self.inner - 1) == 0
        self.late = [0, self.outer // 2]
        self.early = [k for k in range(1, self.outer) if k not in self.late]
        self.blocks = [(k, s) for k in range(self.outer) for s in range(self.inner)]

    def place(self, k, s):
        me = lax.axis_index("modes")
        out = lax.rem(me // self.inner + (k + self.outer), self.outer)
        return out * self.inner + jnp.bitwise_xor(lax.rem(me, self.inner), s)

    def sent(self, k, s, early, late):
        if k in self.late:
            return late[s].at[self.late.index(k)]
        return early[self.early.index(k)].at[s]

    def shapes(self, share):
        early = [(self.inner,) + share] * len(self.early)
        return early + [(len(self.late),) + share] * self.inner

    def divide(self, arrays):
        return arrays[: len(self.early)], arrays[len(self.early) :]

    def got(self, refs):
        inner = self.inner
        late, middle, early = refs[:inner], refs[inner], refs[inner + 1 :]
        found = {(0, s): late[s].at[0] for s in range(inner)}
        found.update({(self.late[1], s): middle.at[s] for s in range(inner)})
        for at, k in enumerate(self.early):
            found.update({(k, s): early[s].at[at] for s in range(inner)})
        return found

    def swap(self, early, late):
        parts = self.outer * self.inner

        def onward(value, k):
            steps = [(d, (d + k * self.inner) % parts) for d in range(parts)]
            return lax.ppermute(value, "modes", steps)

        def across(values):
            pairs = lambda s: [(d, d ^ s) for d in range(parts)]
            return values[:1] + [
                lax.ppermute(value, "modes", pairs(s)) for s, value in enumerate(values) if s
            ]

        early = [onward(value, k) for k, value in zip(self.early, early)]
        late = across(list(late))
        middle = onward(jnp.stack([value[1] for value in late]), self.late[1])
        early = across([jnp.stack([value[s] for value in early]) for s in range(self.inner)])
        return late + [middle] + early


def operator(layout, depth):
    outer, inner = layout.outer, layout.inner
    length = outer * inner * depth
    half = length // 2
    waves = np.arange(half + 1)
    weights = np.where((waves == 0) | (waves == half), 1.0, 2.0) / length
    sigma = 1.0 + (8.0 * waves / length) ** 2
    phases = (np.arange(length)[:, None] * waves[None, :]) % length
    row = (np.cos(phases * (2.0 * np.pi / length)) * (weights * sigma)).sum(1)
    step, slot, plane = np.meshgrid(np.arange(outer), np.arange(inner), np.arange(depth), indexing="ij")
    step, slot, plane = step.ravel(), slot.ravel(), plane.ravel()
    place = np.arange(inner)[:, None]
    sent = (step * inner + (place ^ slot)) * depth + plane
    got = (-step * inner + (place ^ slot)) * depth + plane
    full = row[(sent[:, :, None] - got[:, None, :]) % length].astype(np.float32)
    high = full.astype(jnp.bfloat16)
    low = (full - high.astype(np.float32)).astype(jnp.bfloat16)
    return np.concatenate([high, low], axis=1)


def selector(slots):
    slot = lax.broadcasted_iota(jnp.int32, (LANES, LANES), 0)
    return jnp.where(slot == slots, 1.0, 0.0).astype(f32)


def lane_index(depth):
    return lax.broadcasted_iota(jnp.int32, (depth, LANES), 1)


def roll(value, shift):
    shift = shift % LANES
    return value if shift == 0 else pltpu.roll(value, shift, 1)


def gather_face(column, origin):
    lane = lane_index(column[0].shape[0])
    face = jnp.where(lane == FACE, roll(column[SIDE], FACE - origin - EY + 1), 0.0)
    for j in range(SIDE):
        face = jnp.where(lane // EY == j, roll(column[j], EY * j - origin), face)
    return face


def prepare(terms, slots_ref, mats_ref, geo_ref, left_ref, cells_ref):
    select = selector(slots_ref[...])
    geo = jnp.dot(geo_ref[...], select, precision=lax.Precision.HIGHEST, preferred_element_type=f32)
    left_ref[...] = jnp.zeros_like(left_ref)
    for place, term in enumerate(terms):
        high, low = split(mats_ref[:, term, :])
        left_ref[place, :NODES, 0:NODES] = high
        left_ref[place, :NODES, DEEP : DEEP + NODES] = high
        left_ref[place, :NODES, 2 * DEEP : 2 * DEEP + NODES] = low
    depth = cells_ref.shape[1] // DEEP
    cells_ref[:, NODES * depth :, :] = jnp.zeros((2, (DEEP - NODES) * depth, LANES), f32)
    return select.astype(bf16), geo


def component(terms, first, second, select, geo, left, cells_ref, nodes_ref, inner, extra):
    depth = first.shape[1]
    product = (first[...] * second[...]).reshape(NODES * depth, LANES)
    for place, part in enumerate(split(product)):
        cells_ref[place, : NODES * depth, :] = jnp.dot(part, select, preferred_element_type=f32)
    for pair in range(depth // 2):
        parts = [
            jnp.concatenate(
                [cells_ref[k, pl.ds(2 * pair + p, DEEP, stride=depth), :] for p in (0, 1)], axis=1
            ).astype(bf16)
            for k in (0, 1)
        ]
        right = jnp.concatenate([parts[0], parts[1], parts[0]], axis=0)
        images = jnp.dot(left, right, preferred_element_type=f32)
        for p in (0, 1):
            total = 0.0
            for t, term in enumerate(terms):
                total = total + (
                    images[DEEP * t : DEEP * t + 88, LANES * p : LANES * p + LANES]
                    * geo[term : term + 1]
                )
            nodes_ref[pl.ds(2 * pair + p, 88, stride=depth), :] = total
    lane = lane_index(depth)
    across = lane % EY

    def node(i, j):
        value = nodes_ref[(9 * i + j) * depth : (9 * i + j + 1) * depth, :]
        if i > 0:
            return value
        return value + jnp.where(lane >= EY, roll(node(8, j), EY), 0.0)

    def join(low, high):
        return low + jnp.where(across > 0, roll(high, 1), 0.0)

    end = jnp.zeros((depth, LANES), f32)
    for i in range(SIDE + 1):
        column = [node(i, j) for j in range(SIDE + 1)]
        column[0] = join(column[0], column[SIDE])
        if i < SIDE:
            for j in range(SIDE):
                inner(SIDE * (i - 1) + j, column[j]) if i else extra(j, column[j])
            end = jnp.where(across == i, roll(column[SIDE], i + 1 - EY), end)
        if i in (0, SIDE):
            extra(RIGHT if i else LEFT, gather_face(column, LANES - EY if i else 0))
    extra(ACROSS, end)


def element_kernel(terms, layout, count, *refs):
    vel_hbm, slots_hbm, mats_hbm, geo_hbm = refs[:4]
    outs, scratch = refs[4 : 4 + count], refs[4 + count :]
    vel_ref, slots_ref, mats_ref, geo_ref, left_ref, cells_ref, nodes_ref, sems = scratch[:8]
    out_ref = scratch[8] if layout else outs[0]
    pairs = [(slots_hbm, slots_ref), (geo_hbm, geo_ref), (mats_hbm, mats_ref)]
    pairs += [(vel_hbm.at[c], vel_ref.at[c]) for c in range(3)]
    copies = [pltpu.make_async_copy(*pair, sems.at[k]) for k, pair in enumerate(pairs)]
    for copy in copies:
        copy.start()
    for copy in copies[:3]:
        copy.wait()
    select, geo = prepare(terms, slots_ref, mats_ref, geo_ref, left_ref, cells_ref)
    left = left_ref[...].reshape(len(terms) * DEEP, 3 * DEEP)

    def put(first, row, value):
        out_ref[first + row] = value

    copies[3].wait()
    for c in range(3):
        if c < 2:
            copies[4 + c].wait()
        component(
            terms,
            vel_ref.at[c],
            vel_ref.at[(c + 1) % 3],
            select,
            geo,
            left,
            cells_ref,
            nodes_ref,
            functools.partial(put, c * INNER),
            functools.partial(put, 3 * INNER + c * EXTRA),
        )
    for row in range(3 * (INNER + EXTRA), out_ref.shape[0]):
        out_ref[row] = jnp.zeros(out_ref.shape[1:], f32)
    if layout:
        send_sems = scratch[9]
        share = out_ref.shape[0] // len(layout.blocks)
        early, late = layout.divide(outs)
        copies = [
            pltpu.make_async_copy(
                out_ref.at[pl.ds(layout.place(k, s) * share, share)],
                layout.sent(k, s, early, late),
                send_sems.at[at],
            )
            for at, (k, s) in enumerate(layout.blocks)
        ]
        for copy in copies:
            copy.start()
        for copy in copies:
            copy.wait()


def elements(name, terms, layout, rows, args):
    depth = args[0].shape[2]
    scratch = [
        *(pltpu.VMEM(a.shape, a.dtype) for a in args),
        pltpu.VMEM((len(terms), DEEP, 3 * DEEP), bf16),
        pltpu.VMEM((2, DEEP * depth, LANES), f32),
        pltpu.VMEM((88 * depth, LANES), f32),
        pltpu.SemaphoreType.DMA((6,)),
    ]
    shapes = [(rows, depth, LANES)]
    if layout:
        scratch += [pltpu.VMEM(shapes[0], f32), pltpu.SemaphoreType.DMA((len(layout.blocks),))]
        shapes = layout.shapes((rows // len(layout.blocks), depth, LANES))
    anywhere = pl.BlockSpec(memory_space=pl.ANY)
    return pl.pallas_call(
        functools.partial(element_kernel, terms, layout, len(shapes)),
        in_specs=[anywhere] * len(args),
        out_specs=[anywhere if layout else pl.BlockSpec(memory_space=pltpu.VMEM)] * len(shapes),
        out_shape=[jax.ShapeDtypeStruct(shape, f32) for shape in shapes],
        scratch_shapes=scratch,
        compiler_params=pltpu.CompilerParams(vmem_limit_bytes=WIDE if layout else VMEM),
        cost_estimate=pl.CostEstimate(
            flops=2 * 3 * depth * len(terms) * DEEP * 3 * DEEP * LANES,
            bytes_accessed=4 * 3 * depth * LANES * 150,
            transcendentals=0,
        ),
        name=name,
    )(*args)


def spanwise_kernel(layout, count, *refs):
    got = layout.got(refs[:count])
    table_ref, early, late = refs[count], *layout.divide(refs[count + 1 :])
    share, depth, lanes = late[0].shape[1:]
    length = len(layout.blocks) * depth
    table = table_ref[...]
    for r in range(0, share, 2):
        width = min(2, share - r)
        x = [
            jnp.concatenate([got[block][r + k] for block in layout.blocks], axis=0)
            for k in range(width)
        ]
        x = x[0] if width == 1 else jnp.concatenate(x, axis=1)
        x_high, x_low = split(x)
        y = jnp.dot(table, x_high, preferred_element_type=f32)
        y = y[:length] + y[length:]
        y += jnp.dot(table[:length], x_low, preferred_element_type=f32)
        for at, block in enumerate(layout.blocks):
            for k in range(width):
                layout.sent(*block, early, late)[r + k] = y[
                    depth * at : depth * at + depth, lanes * k : lanes * k + lanes
                ]


def spanwise(layout, values, table):
    share = values[0].shape[1:]
    length = len(layout.blocks) * share[1]
    return pl.pallas_call(
        functools.partial(spanwise_kernel, layout, len(values)),
        out_shape=[jax.ShapeDtypeStruct(shape, f32) for shape in layout.shapes(share)],
        compiler_params=pltpu.CompilerParams(vmem_limit_bytes=VMEM),
        cost_estimate=pl.CostEstimate(
            flops=6 * length * length * share[0] * LANES,
            bytes_accessed=8 * length * share[0] * LANES,
            transcendentals=0,
        ),
        name="spanwise",
    )(*values, table)


def total_kernel(layout, u_ref, *refs):
    total_ref, faces_ref = refs[-2:]
    for (k, s), ref in layout.got(refs[:-2]).items():
        share = ref.shape[0]
        rows = pl.ds(layout.place(-k, s) * share, share)
        total_ref[rows] = u_ref[rows] + ref[...]
    for place, row in enumerate((RIGHT, LEFT)):
        for c in range(3):
            faces_ref[place, c] = total_ref[3 * INNER + c * EXTRA + row]


def totals(layout, u, values):
    return pl.pallas_call(
        functools.partial(total_kernel, layout),
        out_shape=[
            jax.ShapeDtypeStruct(u.shape, f32),
            jax.ShapeDtypeStruct((2, 3) + u.shape[1:], f32),
        ],
        compiler_params=pltpu.CompilerParams(vmem_limit_bytes=VMEM),
        cost_estimate=pl.CostEstimate(flops=u.size, bytes_accessed=12 * u.size, transcendentals=0),
        name="totals",
    )(u, *values)


def to_slots(nodes, select):
    return lax.dot_general(nodes, select, (((1,), (1,)), ((), ())), preferred_element_type=f32)


def pair_selector(slots_ref):
    select = selector(slots_ref[...]).astype(bf16)
    return jnp.concatenate([select, select], axis=1)


def middle_kernel(t_ref, slots_ref, out_ref, nodes_ref, slots_out_ref, sems):
    depth, lanes = t_ref.shape[1:]
    select = pair_selector(slots_ref)
    across = lane_index(depth) % EY
    count = (SIDE - 1) * (SIDE + 1)
    copies = []
    for c in range(3):
        end = t_ref[3 * INNER + c * EXTRA + ACROSS]

        def put(at, value):
            high, low = split(value)
            nodes_ref[pl.ds(at * depth, depth), :] = jnp.concatenate([high, low], axis=1)

        for i in range(1, SIDE):
            for j in range(SIDE):
                value = t_ref[c * INNER + SIDE * (i - 1) + j]
                put((SIDE + 1) * (i - 1) + j, value)
                if j == 0:
                    last = jnp.where(across == EY - 1, roll(end, EY - 1 - i), roll(value, -1))
                    put((SIDE + 1) * (i - 1) + SIDE, last)
        slots_out_ref[c] = to_slots(nodes_ref[...], select).reshape(count, depth, lanes)
        copy = pltpu.make_async_copy(
            slots_out_ref.at[c], out_ref.at[c, pl.ds(SIDE + 1, count)], sems.at[c]
        )
        copy.start()
        copies.append(copy)
    for copy in copies:
        copy.wait()


def faces_kernel(
    t_ref, before_ref, after_ref, slots_ref, _, out_ref, nodes_ref, slots_out_ref, sems
):
    depth, lanes = t_ref.shape[1:]
    select = pair_selector(slots_ref)
    lane = lane_index(depth)
    across = lane % EY
    count = SIDE + 1
    copies = []
    for c in range(3):
        extra = lambda k: t_ref[3 * INNER + c * EXTRA + k]
        before = before_ref[c]
        face = extra(RIGHT) + after_ref[c]
        end = extra(ACROSS) + jnp.where(lane == 0, roll(before, -FACE), 0.0)

        def put(at, value):
            high, low = split(value)
            nodes_ref[pl.ds(at * depth, depth), :] = jnp.concatenate([high, low], axis=1)

        for j in range(SIDE):
            value = extra(j) + jnp.where(lane < EY, roll(before, -EY * j), 0.0)
            moved = roll(face, lanes - EY - EY * j)
            beyond = jnp.where(lane >= lanes - EY, moved, roll(value, -EY))
            put(j, value)
            put(count + j, beyond)
            if j == 0:
                last = jnp.where(across == EY - 1, roll(end, EY - 1), roll(value, -1))
                put(SIDE, last)
                corner = jnp.where(across == EY - 1, roll(end, -1), roll(beyond, -1))
                corner = jnp.where(lane == lanes - 1, roll(face, lanes - 1 - FACE), corner)
                put(count + SIDE, corner)
        slots_out_ref[c] = to_slots(nodes_ref[...], select).reshape(2, count, depth, lanes)
        for side in range(2):
            copy = pltpu.make_async_copy(
                slots_out_ref.at[c, side],
                out_ref.at[c, pl.ds(side * (NODES - count), count)],
                sems.at[c, side],
            )
            copy.start()
            copies.append(copy)
    for copy in copies:
        copy.wait()


def expand(kernel, name, nodes, args, result=None):
    depth = args[0].shape[1]
    shape = (3, *nodes, depth, LANES)
    count = math.prod(nodes)
    vmem = pl.BlockSpec(memory_space=pltpu.VMEM)
    in_specs = [vmem] * len(args)
    aliases = {}
    if result is not None:
        aliases = {len(args): 0}
        args = (*args, result)
        in_specs.append(pl.BlockSpec(memory_space=pl.ANY))
    return pl.pallas_call(
        kernel,
        in_specs=in_specs,
        out_specs=pl.BlockSpec(memory_space=pl.ANY),
        out_shape=jax.ShapeDtypeStruct((3, NODES, depth, LANES), f32),
        scratch_shapes=[
            pltpu.VMEM((count * depth, 2 * LANES), bf16),
            pltpu.VMEM(shape, f32),
            pltpu.SemaphoreType.DMA((3,) + tuple(nodes[:-1])),
        ],
        input_output_aliases=aliases,
        compiler_params=pltpu.CompilerParams(vmem_limit_bytes=VMEM),
        cost_estimate=pl.CostEstimate(
            flops=2 * 3 * count * depth * 256 * 128,
            bytes_accessed=4 * 3 * depth * LANES * 4 * count,
            transcendentals=0,
        ),
        name=name,
    )(*args)


def local(velocity, slot_of_cell, elem_mats, geometry):
    depth = velocity.shape[1]
    parts = lax.axis_size("modes")
    layout = Layout(parts)
    rows = -(-3 * (INNER + EXTRA) // parts) * parts
    args = (velocity.transpose(0, 2, 1, 3), slot_of_cell, elem_mats.transpose(1, 0, 2), geometry)
    table = jnp.asarray(operator(layout, depth))
    table = lax.dynamic_index_in_dim(
        table, lax.rem(lax.axis_index("modes"), layout.inner), keepdims=False
    )
    z = elements("mass", (3,), layout, rows, args)
    pencil = layout.swap(*layout.divide(z))
    (u,) = elements("stiff", (0, 1, 2), None, rows, args)
    y = layout.swap(*layout.divide(spanwise(layout, pencil, table)))
    total, faces = totals(layout, u, y)
    count = lax.axis_size("dom")
    onward = [(k, (k + 1) % count) for k in range(count)]
    back = [(k, (k - 1) % count) for k in range(count)]
    if onward == back:
        before, after = lax.ppermute(faces, "dom", onward)
    else:
        before, after = lax.ppermute(faces[0], "dom", onward), lax.ppermute(faces[1], "dom", back)
    result = expand(middle_kernel, "middle", ((SIDE - 1) * (SIDE + 1),), (total, slot_of_cell))
    args = (total, before, after, slot_of_cell)
    result = expand(faces_kernel, "faces", (2, SIDE + 1), args, result)
    return result.transpose(0, 2, 1, 3)


def solution(mesh):
    in_specs = (P(None, "modes", None, "dom"), P("dom", None), P(), P(None, "dom"))
    out_specs = P(None, "modes", None, "dom")
    return jax.shard_map(local, mesh=mesh, in_specs=in_specs, out_specs=out_specs, check_vma=False)
```

```python
import functools
import math

import jax
import jax.numpy as jnp
import numpy as np
from jax import lax
from jax.experimental import pallas as pl
from jax.experimental.pallas import tpu as pltpu
from jax.sharding import PartitionSpec as P

EX = 16
EY = 8
LANES = EX * EY
NODES = 81
SIDE = 8
INNER = SIDE * (SIDE - 1)
FACE = SIDE * EY
FULL = SIDE * SIDE
ENDS = 3 * FULL
HALF = LANES // 2
HALVES = 10
DEEP = 96
TALL = 88
VMEM = 48 * 1024 * 1024
WIDE = 60 * 1024 * 1024

f32 = jnp.float32
bf16 = jnp.bfloat16


def split(values):
    high = values.astype(bf16)
    return high, (values - high.astype(f32)).astype(bf16)


class Layout:

    def __init__(self, parts):
        self.outer = max(d for d in range(1, math.isqrt(parts) + 1) if parts % d == 0)
        self.inner = parts // self.outer
        assert self.inner & (self.inner - 1) == 0
        self.late = [0, self.outer // 2]
        self.early = [k for k in range(1, self.outer) if k not in self.late]
        self.blocks = [(k, s) for k in range(self.outer) for s in range(self.inner)]

    def place(self, k, s):
        me = lax.axis_index("modes")
        out = lax.rem(me // self.inner + (k + self.outer), self.outer)
        return out * self.inner + jnp.bitwise_xor(lax.rem(me, self.inner), s)

    def sent(self, k, s, early, late):
        if k in self.late:
            return late[s].at[self.late.index(k)]
        return early[self.early.index(k)].at[s]

    def shapes(self, share):
        early = [(self.inner,) + share] * len(self.early)
        return early + [(len(self.late),) + share] * self.inner

    def divide(self, arrays):
        return arrays[: len(self.early)], arrays[len(self.early) :]

    def got(self, refs):
        inner = self.inner
        late, middle, early = refs[:inner], refs[inner], refs[inner + 1 :]
        found = {(0, s): late[s].at[0] for s in range(inner)}
        found.update({(self.late[1], s): middle.at[s] for s in range(inner)})
        for at, k in enumerate(self.early):
            found.update({(k, s): early[s].at[at] for s in range(inner)})
        return found

    def swap(self, early, late):
        parts = self.outer * self.inner

        def onward(value, k):
            steps = [(d, (d + k * self.inner) % parts) for d in range(parts)]
            return lax.ppermute(value, "modes", steps)

        def across(values):
            pairs = lambda s: [(d, d ^ s) for d in range(parts)]
            return values[:1] + [
                lax.ppermute(value, "modes", pairs(s)) for s, value in enumerate(values) if s
            ]

        early = [onward(value, k) for k, value in zip(self.early, early)]
        late = across(list(late))
        middle = onward(jnp.stack([value[1] for value in late]), self.late[1])
        early = across([jnp.stack([value[s] for value in early]) for s in range(self.inner)])
        return late + [middle] + early


def operator(layout, depth):
    outer, inner = layout.outer, layout.inner
    length = outer * inner * depth
    half = length // 2
    waves = np.arange(half + 1)
    weights = np.where((waves == 0) | (waves == half), 1.0, 2.0) / length
    sigma = 1.0 + (8.0 * waves / length) ** 2
    phases = (np.arange(length)[:, None] * waves[None, :]) % length
    row = (np.cos(phases * (2.0 * np.pi / length)) * (weights * sigma)).sum(1)
    step, slot, plane = np.meshgrid(np.arange(outer), np.arange(inner), np.arange(depth), indexing="ij")
    step, slot, plane = step.ravel(), slot.ravel(), plane.ravel()
    place = np.arange(inner)[:, None]
    sent = (step * inner + (place ^ slot)) * depth + plane
    got = (-step * inner + (place ^ slot)) * depth + plane
    full = row[(sent[:, :, None] - got[:, None, :]) % length].astype(np.float32)
    high = full.astype(jnp.bfloat16)
    low = (full - high.astype(np.float32)).astype(jnp.bfloat16)
    return np.concatenate([high, low], axis=1)


def selector(slots):
    slot = lax.broadcasted_iota(jnp.int32, (LANES, LANES), 0)
    return jnp.where(slot == slots, 1.0, 0.0).astype(f32)


def lane_index(depth):
    return lax.broadcasted_iota(jnp.int32, (depth, LANES), 1)


def roll(value, shift):
    shift = shift % LANES
    return value if shift == 0 else pltpu.roll(value, shift, 1)


def gather_face(column, origin):
    lane = lane_index(column[0].shape[0])
    face = jnp.where(lane == FACE, roll(column[SIDE], FACE - origin - EY + 1), 0.0)
    for j in range(SIDE):
        face = jnp.where(lane // EY == j, roll(column[j], EY * j - origin), face)
    return face


def prepare(terms, slots_ref, mats_ref, left_ref):
    select = selector(slots_ref[...]).astype(bf16)
    left_ref[...] = jnp.zeros_like(left_ref)
    for place, term in enumerate(terms):
        high, low = split(mats_ref[:, term, :])
        left_ref[place, :NODES, 0:NODES] = high
        left_ref[place, :NODES, NODES : NODES + 1] = low[:, NODES - 1 :]
        left_ref[place, :NODES, TALL : TALL + NODES] = high
        left_ref[place, :NODES, 2 * TALL :] = low[:, : NODES - 1]
    return jnp.concatenate([select, select], axis=0)


def component(terms, first, second, select, geo, left, scratch, row, ends, face):
    values_ref, images_ref, cells_ref = scratch
    depth = first.shape[1]
    count = NODES * depth
    values_ref[:count] = (first[...] * second[...]).reshape(count, LANES)
    values_ref[count : count + depth] = values_ref[count - depth : count]
    for pair in range(0, depth, 2):
        right = []
        for p in (pair, pair + 1):
            value = values_ref[pl.ds(p, TALL, stride=depth), :]
            high = value.astype(bf16).astype(f32)
            parts = jnp.concatenate([high, value - high, high[: NODES - 1]], axis=0)
            right.append(parts.astype(bf16))
        images = jnp.dot(left, jnp.concatenate(right, axis=1), preferred_element_type=f32)
        for p in (0, 1):
            total = 0.0
            for t, term in enumerate(terms):
                total = total + (
                    images[DEEP * t : DEEP * t + DEEP, LANES * p : LANES * p + LANES]
                    * geo[term : term + 1]
                )
            high, low = split(total)
            images_ref[(pair + p) * DEEP : (pair + p + 1) * DEEP, :LANES] = high
            images_ref[(pair + p) * DEEP : (pair + p + 1) * DEEP, LANES:] = low
    cells_ref[...] = jnp.dot(images_ref[...], select, preferred_element_type=f32)
    lane = lane_index(depth)
    across = lane % EY

    def node(i, j):
        value = cells_ref[pl.ds((SIDE + 1) * i + j, depth, stride=DEEP), :]
        if i > 0:
            return value
        return value + jnp.where(lane >= EY, roll(node(8, j), EY), 0.0)

    def join(low, high):
        return low + jnp.where(across > 0, roll(high, 1), 0.0)

    end = jnp.zeros((depth, LANES), f32)
    for i in range(SIDE + 1):
        column = [node(i, j) for j in range(SIDE + 1)]
        column[0] = join(column[0], column[SIDE])
        if i < SIDE:
            for j in range(SIDE):
                row(SIDE * (i - 1) + j if i else INNER + j, column[j])
            end = jnp.where(across == i, roll(column[SIDE], i + 1 - EY), end)
    ends(end)
    face(gather_face(column, LANES - EY))


def pack(value, half):
    lane = lane_index(value.shape[0] // 2)
    top, bottom = value[: value.shape[0] // 2], value[value.shape[0] // 2 :]
    if half:
        return jnp.where(lane < HALF, roll(top, HALF), bottom)
    return jnp.where(lane < HALF, top, roll(bottom, HALF))


def unpack(packed):
    return jnp.concatenate([packed, roll(packed, HALF)], axis=0)


def element_kernel(terms, layout, count, *refs):
    vel_hbm, slots_hbm, mats_hbm, geo_hbm = refs[:4]
    outs, scratch = refs[4 : 4 + count], refs[4 + count :]
    vel_ref, slots_ref, mats_ref, geo_ref, left_ref, *parts, sems = scratch[:9]
    pairs = [(slots_hbm, slots_ref), (geo_hbm, geo_ref), (mats_hbm, mats_ref)]
    pairs += [(vel_hbm.at[c], vel_ref.at[c]) for c in range(3)]
    copies = [pltpu.make_async_copy(*pair, sems.at[k]) for k, pair in enumerate(pairs)]
    for copy in copies:
        copy.start()
    depth = vel_ref.shape[2]
    spare = (TALL - NODES) * depth
    parts[0][NODES * depth :] = jnp.zeros((spare, LANES), f32)
    for copy in copies[:3]:
        copy.wait()
    select = prepare(terms, slots_ref, mats_ref, left_ref)
    left = left_ref[...].reshape(len(terms) * DEEP, 2 * LANES)
    geo = geo_ref[...]
    if layout:
        rows_ref, halves_ref, send_sems = scratch[9:]
        halves_ref[...] = jnp.zeros_like(halves_ref)
    else:
        (out_ref,) = outs
    lane = lane_index(depth)
    corners = [jnp.zeros((depth, LANES), f32)]

    def put_row(c, row, value):
        if layout:
            rows_ref[(c * FULL + row) * depth : (c * FULL + row + 1) * depth] = value
        else:
            out_ref[c * FULL + row] = value

    def put_half(at, value):
        halves_ref[at * depth // 2 : (at + 1) * depth // 2] = value

    def put_ends(c, value):
        if layout:
            put_half(2 * c, pack(value, 0))
            put_half(2 * c + 1, pack(value, 1))
        else:
            out_ref[ENDS + 2 * c] = value

    def put_face(c, value):
        if layout:
            put_half(6 + c, pack(value, 0))
            corners[0] = jnp.where(lane == c, roll(value, c - FACE), corners[0])
        else:
            out_ref[ENDS + 2 * c + 1] = value

    sends = []
    if layout:
        early, late = layout.divide(outs)
        for k, s in layout.blocks:
            place, target, done = layout.place(k, s), layout.sent(k, s, early, late), 0
            for ref in (rows_ref, halves_ref):
                size = ref.shape[0] // len(layout.blocks)
                source = ref.at[pl.ds(pl.multiple_of(place * size, 8), size)]
                sem = send_sems.at[len(sends)]
                target_part = target.at[pl.ds(done, size)]
                sends.append((place, pltpu.make_async_copy(source, target_part, sem)))
                done += size

    copies[3].wait()
    ready = 0
    for c in range(3):
        if c < 2:
            copies[4 + c].wait()
        puts = [functools.partial(put, c) for put in (put_row, put_ends, put_face)]
        first, second = vel_ref.at[c], vel_ref.at[(c + 1) % 3]
        component(terms, first, second, select, geo, left, parts, *puts)
        if layout:
            before, ready = ready, (c + 1) * FULL * depth * len(layout.blocks) // rows_ref.shape[0]
            ready = len(layout.blocks) if c == 2 else ready
            for place, copy in sends[::2]:
                pl.when(jnp.logical_and(place >= before, place < ready))(copy.start)
    if layout:
        put_half(9, pack(corners[0], 0))
        for _, copy in sends[1::2]:
            copy.start()
        for _, copy in sends:
            copy.wait()


def shares(parts, depth):
    return -(-ENDS // parts) * depth, -(-HALVES // parts) * depth // 2


def elements(name, terms, layout, args):
    depth = args[0].shape[2]
    scratch = [
        *(pltpu.VMEM(a.shape, a.dtype) for a in args),
        pltpu.VMEM((len(terms), DEEP, 2 * LANES), bf16),
        pltpu.VMEM((TALL * depth, LANES), f32),
        pltpu.VMEM((DEEP * depth, 2 * LANES), bf16),
        pltpu.VMEM((DEEP * depth, LANES), f32),
        pltpu.SemaphoreType.DMA((6,)),
    ]
    shapes = [(ENDS + 6, depth, LANES)]
    if layout:
        sizes = shares(len(layout.blocks), depth)
        scratch += [pltpu.VMEM((len(layout.blocks) * size, LANES), f32) for size in sizes]
        scratch.append(pltpu.SemaphoreType.DMA((2 * len(layout.blocks),)))
        shapes = layout.shapes((sum(sizes), LANES))
    anywhere = pl.BlockSpec(memory_space=pl.ANY)
    return pl.pallas_call(
        functools.partial(element_kernel, terms, layout, len(shapes)),
        in_specs=[anywhere] * len(args),
        out_specs=[anywhere if layout else pl.BlockSpec(memory_space=pltpu.VMEM)] * len(shapes),
        out_shape=[jax.ShapeDtypeStruct(shape, f32) for shape in shapes],
        scratch_shapes=scratch,
        compiler_params=pltpu.CompilerParams(vmem_limit_bytes=WIDE if layout else VMEM),
        cost_estimate=pl.CostEstimate(
            flops=2 * 3 * depth * len(terms) * DEEP * 3 * DEEP * LANES,
            bytes_accessed=4 * 3 * depth * LANES * 150,
            transcendentals=0,
        ),
        name=name,
    )(*args)


def spanwise_kernel(layout, depth, count, *refs):
    got = layout.got(refs[:count])
    table_ref, early, late = refs[count], *layout.divide(refs[count + 1 :])
    full, _ = shares(len(layout.blocks), depth)
    length = len(layout.blocks) * depth
    table = table_ref[...]
    rows = [(at, depth) for at in range(0, full, depth)]
    rows += [(at, depth // 2) for at in range(full, late[0].shape[1], depth // 2)]
    for first in range(0, len(rows), 2):
        group = rows[first : first + 2]
        x = []
        for at, size in group:
            blocks = [got[block][at : at + size] for block in layout.blocks]
            if size < depth:
                blocks = [unpack(block) for block in blocks]
            x.append(jnp.concatenate(blocks, axis=0))
        x_high, x_low = split(jnp.concatenate(x, axis=1))
        y = jnp.dot(table, x_high, preferred_element_type=f32)
        y = y[:length] + y[length:]
        y += jnp.dot(table[:length], x_low, preferred_element_type=f32)
        for place, block in enumerate(layout.blocks):
            for k, (at, size) in enumerate(group):
                value = y[depth * place : depth * place + depth, LANES * k : LANES * k + LANES]
                value = value if size == depth else pack(value, 0)
                layout.sent(*block, early, late)[at : at + size] = value


def spanwise(layout, depth, values, table):
    share = values[0].shape[1:]
    length = len(layout.blocks) * depth
    return pl.pallas_call(
        functools.partial(spanwise_kernel, layout, depth, len(values)),
        out_shape=[jax.ShapeDtypeStruct(shape, f32) for shape in layout.shapes(share)],
        compiler_params=pltpu.CompilerParams(vmem_limit_bytes=VMEM),
        cost_estimate=pl.CostEstimate(
            flops=6 * length * len(layout.blocks) * share[0] * LANES,
            bytes_accessed=8 * len(layout.blocks) * share[0] * LANES,
            transcendentals=0,
        ),
        name="spanwise",
    )(*values, table)


def total_kernel(layout, u_ref, *refs):
    total_ref, faces_ref, rows_ref, halves_ref = refs[-4:]
    depth = u_ref.shape[1]
    full, half = shares(len(layout.blocks), depth)
    for (k, s), ref in layout.got(refs[:-4]).items():
        place = layout.place(-k, s)
        rows_ref[pl.ds(place * (full // depth), full // depth)] = ref[:full].reshape(
            full // depth, depth, LANES
        )
        halves_ref[pl.ds(pl.multiple_of(place * half, 8), half)] = ref[full:]
    total_ref[:ENDS] = u_ref[:ENDS] + rows_ref[:ENDS]
    lane = lane_index(depth)
    halves = [
        unpack(halves_ref[at * depth // 2 : (at + 1) * depth // 2]) for at in range(HALVES)
    ]
    for c in range(3):
        end = jnp.where(lane < HALF, halves[2 * c], roll(halves[2 * c + 1], HALF))
        end += u_ref[ENDS + 2 * c]
        face = jnp.where(lane == FACE, roll(halves[9], FACE - c), halves[6 + c])
        face += u_ref[ENDS + 2 * c + 1]
        total_ref[ENDS + 2 * c] = end
        total_ref[ENDS + 2 * c + 1] = face
        faces_ref[0, c] = face
        column = [total_ref[c * FULL + INNER + j] for j in range(SIDE)]
        faces_ref[1, c] = gather_face(column + [roll(end, EY - 1)], 0)


def totals(layout, u, values):
    depth = u.shape[1]
    full, half = shares(len(layout.blocks), depth)
    return pl.pallas_call(
        functools.partial(total_kernel, layout),
        out_shape=[
            jax.ShapeDtypeStruct(u.shape, f32),
            jax.ShapeDtypeStruct((2, 3, depth, LANES), f32),
        ],
        scratch_shapes=[
            pltpu.VMEM((len(layout.blocks) * full // depth, depth, LANES), f32),
            pltpu.VMEM((len(layout.blocks) * half, LANES), f32),
        ],
        compiler_params=pltpu.CompilerParams(vmem_limit_bytes=VMEM),
        cost_estimate=pl.CostEstimate(flops=u.size, bytes_accessed=12 * u.size, transcendentals=0),
        name="totals",
    )(u, *values)


def to_slots(nodes, select):
    return lax.dot_general(nodes, select, (((1,), (1,)), ((), ())), preferred_element_type=f32)


def pair_selector(slots_ref):
    select = selector(slots_ref[...]).astype(bf16)
    return jnp.concatenate([select, select], axis=1)


def middle_kernel(t_ref, slots_ref, out_ref, nodes_ref, slots_out_ref, sems):
    depth, lanes = t_ref.shape[1:]
    select = pair_selector(slots_ref)
    across = lane_index(depth) % EY
    count = (SIDE - 1) * (SIDE + 1)
    copies = []
    for c in range(3):
        end = t_ref[ENDS + 2 * c]

        def put(at, value):
            high, low = split(value)
            nodes_ref[pl.ds(at * depth, depth), :] = jnp.concatenate([high, low], axis=1)

        for i in range(1, SIDE):
            for j in range(SIDE):
                value = t_ref[c * FULL + SIDE * (i - 1) + j]
                put((SIDE + 1) * (i - 1) + j, value)
                if j == 0:
                    last = jnp.where(across == EY - 1, roll(end, EY - 1 - i), roll(value, -1))
                    put((SIDE + 1) * (i - 1) + SIDE, last)
        slots_out_ref[c] = to_slots(nodes_ref[...], select).reshape(count, depth, lanes)
        copy = pltpu.make_async_copy(
            slots_out_ref.at[c], out_ref.at[c, pl.ds(SIDE + 1, count)], sems.at[c]
        )
        copy.start()
        copies.append(copy)
    for copy in copies:
        copy.wait()


def faces_kernel(
    t_ref, before_ref, after_ref, slots_ref, _, out_ref, nodes_ref, slots_out_ref, sems
):
    depth, lanes = t_ref.shape[1:]
    select = pair_selector(slots_ref)
    lane = lane_index(depth)
    across = lane % EY
    count = SIDE + 1
    copies = []
    for c in range(3):
        before = before_ref[c]
        face = t_ref[ENDS + 2 * c + 1] + after_ref[c]
        end = t_ref[ENDS + 2 * c] + jnp.where(lane == 0, roll(before, -FACE), 0.0)

        def put(at, value):
            high, low = split(value)
            nodes_ref[pl.ds(at * depth, depth), :] = jnp.concatenate([high, low], axis=1)

        for j in range(SIDE):
            value = t_ref[c * FULL + INNER + j] + jnp.where(lane < EY, roll(before, -EY * j), 0.0)
            moved = roll(face, lanes - EY - EY * j)
            beyond = jnp.where(lane >= lanes - EY, moved, roll(value, -EY))
            put(j, value)
            put(count + j, beyond)
            if j == 0:
                last = jnp.where(across == EY - 1, roll(end, EY - 1), roll(value, -1))
                put(SIDE, last)
                corner = jnp.where(across == EY - 1, roll(end, -1), roll(beyond, -1))
                corner = jnp.where(lane == lanes - 1, roll(face, lanes - 1 - FACE), corner)
                put(count + SIDE, corner)
        slots_out_ref[c] = to_slots(nodes_ref[...], select).reshape(2, count, depth, lanes)
        for side in range(2):
            copy = pltpu.make_async_copy(
                slots_out_ref.at[c, side],
                out_ref.at[c, pl.ds(side * (NODES - count), count)],
                sems.at[c, side],
            )
            copy.start()
            copies.append(copy)
    for copy in copies:
        copy.wait()


def expand(kernel, name, nodes, args, result=None):
    depth = args[0].shape[1]
    shape = (3, *nodes, depth, LANES)
    count = math.prod(nodes)
    vmem = pl.BlockSpec(memory_space=pltpu.VMEM)
    in_specs = [vmem] * len(args)
    aliases = {}
    if result is not None:
        aliases = {len(args): 0}
        args = (*args, result)
        in_specs.append(pl.BlockSpec(memory_space=pl.ANY))
    return pl.pallas_call(
        kernel,
        in_specs=in_specs,
        out_specs=pl.BlockSpec(memory_space=pl.ANY),
        out_shape=jax.ShapeDtypeStruct((3, NODES, depth, LANES), f32),
        scratch_shapes=[
            pltpu.VMEM((count * depth, 2 * LANES), bf16),
            pltpu.VMEM(shape, f32),
            pltpu.SemaphoreType.DMA((3,) + tuple(nodes[:-1])),
        ],
        input_output_aliases=aliases,
        compiler_params=pltpu.CompilerParams(vmem_limit_bytes=VMEM),
        cost_estimate=pl.CostEstimate(
            flops=2 * 3 * count * depth * 256 * 128,
            bytes_accessed=4 * 3 * depth * LANES * 4 * count,
            transcendentals=0,
        ),
        name=name,
    )(*args)


def local(velocity, slot_of_cell, elem_mats, geometry):
    depth = velocity.shape[1]
    parts = lax.axis_size("modes")
    layout = Layout(parts)
    args = (velocity.transpose(0, 2, 1, 3), slot_of_cell, elem_mats.transpose(1, 0, 2), geometry)
    table = jnp.asarray(operator(layout, depth))
    table = lax.dynamic_index_in_dim(
        table, lax.rem(lax.axis_index("modes"), layout.inner), keepdims=False
    )
    z = elements("mass", (3,), layout, args)
    pencil = layout.swap(*layout.divide(z))
    (u,) = elements("stiff", (0, 1, 2), None, args)
    y = layout.swap(*layout.divide(spanwise(layout, depth, pencil, table)))
    total, faces = totals(layout, u, y)
    count = lax.axis_size("dom")
    onward = [(k, (k + 1) % count) for k in range(count)]
    back = [(k, (k - 1) % count) for k in range(count)]
    if onward == back:
        before, after = lax.ppermute(faces, "dom", onward)
    else:
        before, after = lax.ppermute(faces[0], "dom", onward), lax.ppermute(faces[1], "dom", back)
    result = expand(middle_kernel, "middle", ((SIDE - 1) * (SIDE + 1),), (total, slot_of_cell))
    args = (total, before, after, slot_of_cell)
    result = expand(faces_kernel, "faces", (2, SIDE + 1), args, result)
    return result.transpose(0, 2, 1, 3)


def solution(mesh):
    in_specs = (P(None, "modes", None, "dom"), P("dom", None), P(), P(None, "dom"))
    out_specs = P(None, "modes", None, "dom")
    return jax.shard_map(local, mesh=mesh, in_specs=in_specs, out_specs=out_specs, check_vma=False)
```

```python
import functools
import math

import jax
import jax.numpy as jnp
import numpy as np
from jax import lax
from jax.experimental import pallas as pl
from jax.experimental.pallas import tpu as pltpu
from jax.sharding import PartitionSpec as P

EX = 16
EY = 8
LANES = EX * EY
NODES = 81
SIDE = 8
INNER = SIDE * (SIDE - 1)
FACE = SIDE * EY
HALF = LANES // 2
ENDS = 3 * SIDE
FACES = ENDS + 3
EXTRAS = FACES + 3
CORNERS = 2 * FACES + 3
HALVES = CORNERS + 1
DEEP = 96
PITCH = 104
TALL = 88
VMEM = 48 * 1024 * 1024
WIDE = 60 * 1024 * 1024

f32 = jnp.float32
bf16 = jnp.bfloat16


def split(values):
    high = values.astype(bf16)
    return high, (values - high.astype(f32)).astype(bf16)


class Layout:

    def __init__(self, parts):
        self.outer = max(d for d in range(1, math.isqrt(parts) + 1) if parts % d == 0)
        self.inner = parts // self.outer
        assert self.inner & (self.inner - 1) == 0
        self.late = [0, self.outer // 2]
        self.early = [k for k in range(1, self.outer) if k not in self.late]
        self.blocks = [(k, s) for k in range(self.outer) for s in range(self.inner)]

    def place(self, k, s):
        me = lax.axis_index("modes")
        out = lax.rem(me // self.inner + (k + self.outer), self.outer)
        return out * self.inner + jnp.bitwise_xor(lax.rem(me, self.inner), s)

    def sent(self, k, s, early, late):
        if k in self.late:
            return late[s].at[self.late.index(k)]
        return early[self.early.index(k)].at[s]

    def share(self, depth):
        count = len(self.blocks)
        full = 3 * INNER // count
        rest = -(-2 * (3 * INNER - full * count) // count)
        if rest == 2:
            full, rest = full + 1, 0
        lower = full // 2
        extra = -(-HALVES // count)
        return lower * depth, extra * depth // 2, (full - lower) * depth, rest * depth // 2

    def base(self, depth):
        return self.share(depth)[0] // depth * len(self.blocks)

    def shapes(self, share):
        early = [(self.inner,) + share] * len(self.early)
        return early + [(len(self.late),) + share] * self.inner

    def divide(self, arrays):
        return arrays[: len(self.early)], arrays[len(self.early) :]

    def got(self, refs):
        inner = self.inner
        late, middle, early = refs[:inner], refs[inner:], refs[inner + len(self.late) - 1 :]
        found = {(0, s): late[s].at[0] for s in range(inner)}
        for at, k in enumerate(self.late[1:]):
            found.update({(k, s): middle[at].at[s] for s in range(inner)})
        for at, k in enumerate(self.early):
            found.update({(k, s): early[s].at[at] for s in range(inner)})
        return found

    def onward(self, value, k):
        parts = self.outer * self.inner
        steps = [(d, (d + k * self.inner) % parts) for d in range(parts)]
        return lax.ppermute(value, "modes", steps)

    def across(self, values):
        pairs = lambda s: [(d, d ^ s) for d in range(self.outer * self.inner)]
        return values[:1] + [
            lax.ppermute(value, "modes", pairs(s)) for s, value in enumerate(values) if s
        ]

    def start(self, early, late):
        early = [self.onward(value, k) for k, value in zip(self.early, early)]
        return early, self.across(list(late))

    def middle(self, late, part=slice(None)):
        return [
            self.onward(jnp.stack([value[at, part] for value in late]), k)
            for at, k in enumerate(self.late)
            if k
        ]

    def end(self, early):
        return self.across([jnp.stack([value[s] for value in early]) for s in range(self.inner)])


def following(values, *earlier):
    return [lax.optimization_barrier((value, *earlier))[0] for value in values]


def operator(layout, depth):
    outer, inner = layout.outer, layout.inner
    length = outer * inner * depth
    half = length // 2
    waves = np.arange(half + 1)
    weights = np.where((waves == 0) | (waves == half), 1.0, 2.0) / length
    sigma = 1.0 + (8.0 * waves / length) ** 2
    phases = (np.arange(length)[:, None] * waves[None, :]) % length
    row = (np.cos(phases * (2.0 * np.pi / length)) * (weights * sigma)).sum(1)
    step, slot, plane = np.meshgrid(np.arange(outer), np.arange(inner), np.arange(depth), indexing="ij")
    step, slot, plane = step.ravel(), slot.ravel(), plane.ravel()
    place = np.arange(inner)[:, None]
    sent = (step * inner + (place ^ slot)) * depth + plane
    got = (-step * inner + (place ^ slot)) * depth + plane
    full = row[(sent[:, :, None] - got[:, None, :]) % length].astype(np.float32)
    high = full.astype(jnp.bfloat16)
    low = (full - high.astype(np.float32)).astype(jnp.bfloat16)
    return np.concatenate([high, low], axis=1)


def selector(slots):
    slot = lax.broadcasted_iota(jnp.int32, (LANES, LANES), 0)
    return jnp.where(slot == slots, 1.0, 0.0).astype(f32)


def lane_index(depth):
    return lax.broadcasted_iota(jnp.int32, (depth, LANES), 1)


def roll(value, shift):
    shift = shift % LANES
    return value if shift == 0 else pltpu.roll(value, shift, 1)


def gather_face(column, origin):
    lane = lane_index(column[0].shape[0])
    face = jnp.where(lane == FACE, roll(column[SIDE], FACE - origin - EY + 1), 0.0)
    for j in range(SIDE):
        face = jnp.where(lane // EY == j, roll(column[j], EY * j - origin), face)
    return face


def prepare(terms, slots_ref, mats_ref, left_ref):
    select = selector(slots_ref[...]).astype(bf16)
    left_ref[...] = jnp.zeros_like(left_ref)
    for place, term in enumerate(terms):
        high, low = split(mats_ref[:, term, :])
        left_ref[place, :NODES, 0:NODES] = high
        left_ref[place, :NODES, NODES : NODES + 1] = low[:, NODES - 1 :]
        left_ref[place, :NODES, TALL : TALL + NODES] = high
        left_ref[place, :NODES, 2 * TALL :] = low[:, : NODES - 1]
    return jnp.concatenate([select, select], axis=0)


def component(terms, first, second, select, geo, left, scratch, row, ends, face):
    values_ref, images_ref, cells_ref = scratch
    depth = first.shape[1]
    values_ref[:NODES, :depth] = first[...] * second[...]
    values_ref[NODES, :depth] = values_ref[NODES - 1, :depth]
    flat = values_ref.reshape(TALL * (depth + 8), LANES)
    for pair in range(0, depth, 2):
        right = []
        for p in (pair, pair + 1):
            value = flat[pl.ds(p, TALL, stride=depth + 8), :]
            high = value.astype(bf16).astype(f32)
            parts = jnp.concatenate([high, value - high, high[: NODES - 1]], axis=0)
            right.append(parts.astype(bf16))
        images = jnp.dot(left, jnp.concatenate(right, axis=1), preferred_element_type=f32)
        for p in (0, 1):
            total = 0.0
            for t, term in enumerate(terms):
                total = total + (
                    images[DEEP * t : DEEP * t + DEEP, LANES * p : LANES * p + LANES]
                    * geo[term : term + 1]
                )
            high, low = split(total)
            images_ref[(pair + p) * DEEP : (pair + p + 1) * DEEP, :LANES] = high
            images_ref[(pair + p) * DEEP : (pair + p + 1) * DEEP, LANES:] = low
    cells = jnp.dot(images_ref[...], select, preferred_element_type=f32)
    for p in range(depth):
        cells_ref[p * PITCH : p * PITCH + DEEP] = cells[p * DEEP : (p + 1) * DEEP]
    lane = lane_index(depth)
    across = lane % EY

    def node(i, j):
        value = cells_ref[pl.ds((SIDE + 1) * i + j, depth, stride=PITCH), :]
        if i > 0:
            return value
        return value + jnp.where(lane >= EY, roll(node(8, j), EY), 0.0)

    def join(low, high):
        return low + jnp.where(across > 0, roll(high, 1), 0.0)

    end = jnp.zeros((depth, LANES), f32)
    for i in range(SIDE + 1):
        column = [node(i, j) for j in range(SIDE + 1)]
        column[0] = join(column[0], column[SIDE])
        if i < SIDE:
            for j in range(SIDE):
                row(SIDE * (i - 1) + j if i else INNER + j, column[j])
            end = jnp.where(across == i, roll(column[SIDE], i + 1 - EY), end)
    ends(end)
    face(gather_face(column, LANES - EY))


def pack(value, half):
    lane = lane_index(value.shape[0] // 2)
    top, bottom = value[: value.shape[0] // 2], value[value.shape[0] // 2 :]
    if half:
        return jnp.where(lane < HALF, roll(top, HALF), bottom)
    return jnp.where(lane < HALF, top, roll(bottom, HALF))


def unpack(packed):
    return jnp.concatenate([packed, roll(packed, HALF)], axis=0)


def element_kernel(terms, layout, count, *refs):
    vel_hbm, slots_hbm, mats_hbm, geo_hbm = refs[:4]
    outs, scratch = refs[4 : 4 + count], refs[4 + count :]
    vel_ref, slots_ref, mats_ref, geo_ref, left_ref, *parts, sems = scratch[:9]
    pairs = [(slots_hbm, slots_ref), (geo_hbm, geo_ref), (mats_hbm, mats_ref)]
    pairs += [(vel_hbm.at[c], vel_ref.at[c]) for c in range(3)]
    copies = [pltpu.make_async_copy(*pair, sems.at[k]) for k, pair in enumerate(pairs)]
    for copy in copies:
        copy.start()
    depth = vel_ref.shape[2]
    parts[0][NODES:] = jnp.zeros((TALL - NODES, depth + 8, LANES), f32)
    sends = []
    corners = [jnp.zeros((depth, LANES), f32)]
    if layout:
        lower_ref, extras_ref, upper_ref, halves_ref, send_sems = scratch[9:]
        halves_ref[...] = jnp.zeros_like(halves_ref)
        extras_ref[...] = jnp.zeros_like(extras_ref)
        early, late = layout.divide(outs)
        sizes, base = layout.share(depth), layout.base(depth)
        full = base + upper_ref.shape[0] // depth
        buffers = ((lower_ref, 0), (extras_ref, None), (upper_ref, base), (halves_ref, None))
        for k, s in layout.blocks:
            place, target, done = layout.place(k, s), layout.sent(k, s, early, late), 0
            for (ref, begin), size in zip(buffers, sizes):
                source = ref.at[pl.ds(pl.multiple_of(place * size, 8), size)]
                if size:
                    target_part = target.at[pl.ds(done, size)]
                    copy = pltpu.make_async_copy(source, target_part, send_sems.at[len(sends)])
                    sends.append((place, begin, size // depth, copy))
                done += size

    def put_half(ref, at, value, half=0):
        ref[at * depth // 2 : (at + 1) * depth // 2] = pack(value, half)

    def put_extra(row, value):
        if layout:
            put_half(extras_ref, 2 * row, value)
            put_half(extras_ref, 2 * row + 1, value, 1)
        else:
            outs[1][row] = value

    def put_row(c, row, value):
        if row >= INNER:
            put_extra(SIDE * c + row - INNER, value)
            return
        row += c * INNER
        if not layout:
            outs[0][row] = value
        elif row < base:
            lower_ref[row * depth : (row + 1) * depth] = value
        elif row < full:
            upper_ref[(row - base) * depth : (row - base + 1) * depth] = value
        else:
            put_half(halves_ref, 2 * (row - full), value)
            put_half(halves_ref, 2 * (row - full) + 1, value, 1)

    def put_end(c, value):
        put_extra(ENDS + c, value)

    def put_face(c, value):
        if layout:
            put_half(extras_ref, 2 * FACES + c, value)
            corners[0] = jnp.where(lane_index(depth) == c, roll(value, c - FACE), corners[0])
        else:
            outs[1][FACES + c] = value

    for copy in copies[:3]:
        copy.wait()
    select = prepare(terms, slots_ref, mats_ref, left_ref)
    left = left_ref[...].reshape(len(terms) * DEEP, 2 * LANES)
    geo = geo_ref[...]
    copies[3].wait()
    for c in range(3):
        if c < 2:
            copies[4 + c].wait()
        puts = [functools.partial(store, c) for store in (put_row, put_end, put_face)]
        first, second = vel_ref.at[c], vel_ref.at[(c + 1) % 3]
        component(terms, first, second, select, geo, left, parts, *puts)
        for place, begin, count, copy in sends:
            if begin is None:
                continue
            blocks = len(layout.blocks)
            before, ready = (
                max(0, min(blocks, (rows - begin) // count)) for rows in (c * INNER, (c + 1) * INNER)
            )
            if before < ready == blocks and before == 0:
                copy.start()
            elif before < ready:
                pl.when(jnp.logical_and(place >= before, place < ready))(copy.start)
    if layout:
        put_half(extras_ref, CORNERS, corners[0])
    for _, begin, _, copy in sends:
        if begin is None:
            copy.start()
    for *_, copy in sends:
        copy.wait()


def elements(name, terms, layout, args):
    depth = args[0].shape[2]
    scratch = [
        *(pltpu.VMEM(a.shape, a.dtype) for a in args),
        pltpu.VMEM((len(terms), DEEP, 2 * LANES), bf16),
        pltpu.VMEM((TALL, depth + 8, LANES), f32),
        pltpu.VMEM((DEEP * depth, 2 * LANES), bf16),
        pltpu.VMEM((PITCH * depth, LANES), f32),
        pltpu.SemaphoreType.DMA((6,)),
    ]
    anywhere, vmem = pl.BlockSpec(memory_space=pl.ANY), pl.BlockSpec(memory_space=pltpu.VMEM)
    shapes, specs = [(3 * INNER, depth, LANES)], [vmem]
    if layout:
        count = len(layout.blocks)
        sizes = layout.share(depth)
        scratch += [pltpu.VMEM((count * max(size, 8), LANES), f32) for size in sizes]
        scratch.append(pltpu.SemaphoreType.DMA((4 * count,)))
        shapes = layout.shapes((sum(sizes), LANES))
        specs = [anywhere] * len(shapes)
    else:
        shapes.append((EXTRAS, depth, LANES))
        specs.append(vmem)
    return pl.pallas_call(
        functools.partial(element_kernel, terms, layout, len(shapes)),
        in_specs=[anywhere] * len(args),
        out_specs=specs,
        out_shape=[jax.ShapeDtypeStruct(shape, f32) for shape in shapes],
        scratch_shapes=scratch,
        compiler_params=pltpu.CompilerParams(vmem_limit_bytes=WIDE if layout else VMEM),
        cost_estimate=pl.CostEstimate(
            flops=2 * 3 * depth * len(terms) * DEEP * 3 * DEEP * LANES,
            bytes_accessed=4 * 3 * depth * LANES * 150,
            transcendentals=0,
        ),
        name=name,
    )(*args)


def left_sums(before, j):
    lane = lane_index(before.shape[0])
    if j < SIDE:
        return jnp.where(lane < EY, roll(before, -EY * j), 0.0)
    return jnp.where(lane == 0, roll(before, -FACE), 0.0)


def spanwise_kernel(layout, depth, count, *refs):
    got = layout.got(refs[:count])
    table_ref, early, late = refs[count], *layout.divide(refs[count + 1 :])
    length = len(layout.blocks) * depth
    table = table_ref[lax.rem(lax.axis_index("modes"), layout.inner)]
    rows, begin = [], 0
    for sublanes, size in zip(layout.share(depth), (depth, depth // 2) * 2):
        rows += [(at, size) for at in range(begin, begin + sublanes, size)]
        begin += sublanes
    for first in range(0, len(rows), 2):
        group = rows[first : first + 2]
        x = []
        for at, size in group:
            blocks = [got[block][at : at + size] for block in layout.blocks]
            if size < depth:
                blocks = [unpack(block) for block in blocks]
            x.append(jnp.concatenate(blocks, axis=0))
        x_high, x_low = split(jnp.concatenate(x, axis=1))
        y = jnp.dot(table, x_high, preferred_element_type=f32)
        y = y[:length] + y[length:]
        y += jnp.dot(table[:length], x_low, preferred_element_type=f32)
        for place, block in enumerate(layout.blocks):
            for k, (at, size) in enumerate(group):
                value = y[depth * place : depth * place + depth, LANES * k : LANES * k + LANES]
                value = value if size == depth else pack(value, 0)
                layout.sent(*block, early, late)[at : at + size] = value


def spanwise(layout, depth, values, table):
    length = len(layout.blocks) * depth
    sizes = layout.share(depth)
    shapes = layout.shapes((sum(sizes), LANES))
    return pl.pallas_call(
        functools.partial(spanwise_kernel, layout, depth, len(values)),
        out_shape=[jax.ShapeDtypeStruct(shape, f32) for shape in shapes],
        compiler_params=pltpu.CompilerParams(vmem_limit_bytes=VMEM),
        cost_estimate=pl.CostEstimate(
            flops=6 * length * len(layout.blocks) * sum(sizes) * LANES,
            bytes_accessed=8 * len(layout.blocks) * sum(sizes) * LANES,
            transcendentals=0,
        ),
        name="spanwise",
    )(*values, table)


def to_slots(nodes, select):
    return lax.dot_general(nodes, select, (((1,), (1,)), ((), ())), preferred_element_type=f32)


def pair_selector(slots_ref):
    select = selector(slots_ref[...]).astype(bf16)
    return jnp.concatenate([select, select], axis=1)


def single(ref, at, depth):
    return unpack(ref[at * depth // 2 : (at + 1) * depth // 2])


def double(ref, at, depth):
    lower, upper = single(ref, at, depth), single(ref, at + 1, depth)
    return jnp.where(lane_index(depth) < HALF, lower, roll(upper, HALF))


def totals_kernel(layout, u_ref, *refs):
    total_ref, faces_ref, halves_ref = refs[-3:]
    depth = u_ref.shape[1]
    begin, size = layout.share(depth)[:2]
    for (k, s), ref in layout.got(refs[:-3]).items():
        at = pl.ds(pl.multiple_of(layout.place(-k, s) * size, 8), size)
        halves_ref[at] = ref[begin : begin + size]
    corners = single(halves_ref, CORNERS, depth)
    lane = lane_index(depth)
    last = jnp.zeros((depth, LANES), f32)
    for c in range(3):
        column = []
        for j in range(SIDE + 1):
            row = ENDS + c if j == SIDE else SIDE * c + j
            column.append(u_ref[row] + double(halves_ref, 2 * row, depth))
            total_ref[row] = column[j]
        face = single(halves_ref, 2 * FACES + c, depth)
        face = jnp.where(lane_index(depth) == FACE, roll(corners, FACE - c), face)
        face += u_ref[FACES + c]
        total_ref[FACES + c] = face
        left = gather_face(column[:SIDE] + [roll(column[SIDE], EY - 1)], 0)
        faces_ref[c] = jnp.where(lane < HALF, face, roll(left, HALF))
        last = jnp.where(lane == c, roll(face, c - FACE), last)
        last = jnp.where(lane == SIDE + c, roll(left, SIDE + c - FACE), last)
    faces_ref[3] = last


def totals(layout, u, values):
    depth = u.shape[1]
    size = layout.share(depth)[1]
    return pl.pallas_call(
        functools.partial(totals_kernel, layout),
        out_shape=[
            jax.ShapeDtypeStruct(u.shape, f32),
            jax.ShapeDtypeStruct((4, depth, LANES), f32),
        ],
        scratch_shapes=[pltpu.VMEM((len(layout.blocks) * size, LANES), f32)],
        compiler_params=pltpu.CompilerParams(vmem_limit_bytes=VMEM),
        cost_estimate=pl.CostEstimate(flops=0, bytes_accessed=0, transcendentals=0),
        name="totals",
    )(u, *values)


def put_node(nodes_ref, depth, at, value):
    high, low = split(value)
    nodes_ref[pl.ds(at * depth, depth), :] = jnp.concatenate([high, low], axis=1)


def faces_kernel(
    t_ref, before_ref, after_ref, slots_ref, _, out_ref, nodes_ref, slots_out_ref, sems
):
    depth, lanes = t_ref.shape[1:]
    select = pair_selector(slots_ref)
    lane = lane_index(depth)
    across = lane % EY
    count = SIDE + 1
    copies = []
    for c in range(3):
        put = functools.partial(put_node, nodes_ref, depth)
        before = jnp.where(lane == FACE, roll(before_ref[3], FACE - c), before_ref[c])
        after = roll(after_ref[c], HALF)
        after = jnp.where(lane == FACE, roll(after_ref[3], FACE - SIDE - c), after)
        face = t_ref[FACES + c] + after
        end = t_ref[ENDS + c] + left_sums(before, SIDE)
        for j in range(SIDE):
            value = t_ref[SIDE * c + j] + left_sums(before, j)
            moved = roll(face, lanes - EY - EY * j)
            beyond = jnp.where(lane >= lanes - EY, moved, roll(value, -EY))
            put(j, value)
            put(count + j, beyond)
            if j == 0:
                last = jnp.where(across == EY - 1, roll(end, EY - 1), roll(value, -1))
                put(SIDE, last)
                corner = jnp.where(across == EY - 1, roll(end, -1), roll(beyond, -1))
                corner = jnp.where(lane == lanes - 1, roll(face, lanes - 1 - FACE), corner)
                put(count + SIDE, corner)
        slots_out_ref[c] = to_slots(nodes_ref[...], select).reshape(2, count, depth, lanes)
        for side in range(2):
            copy = pltpu.make_async_copy(
                slots_out_ref.at[c, side],
                out_ref.at[c, pl.ds(side * (NODES - count), count)],
                sems.at[c, side],
            )
            copy.start()
            copies.append(copy)
    for copy in copies:
        copy.wait()


def middle_groups(layout, depth, upper):
    group = SIDE - 1
    cut = layout.base(depth) // SIDE
    first, last = (cut, 3 * group) if upper else (0, cut)
    groups = []
    while first < last:
        count = min(last - first, group - first % group)
        groups.append((first // group, first % group + 1, count))
        first += count
    return groups


def middle_kernel(layout, upper, u_ref, t_ref, slots_ref, *refs):
    values = refs[: -7 if upper else -6]
    out_ref, nodes_ref, slots_out_ref, sems, rows_ref, halves_ref = refs[-6:]
    depth, lanes = u_ref.shape[1:]
    sizes = layout.share(depth)
    full, half = sizes[2:] if upper else (sizes[0], 0)
    base = layout.base(depth) if upper else 0
    whole = full // depth
    for (k, s), ref in layout.got(values).items():
        place = layout.place(-k, s)
        begin = sum(sizes[:2]) if upper and k != layout.late[1] else 0
        rows_ref[pl.ds(place * whole, whole)] = ref[begin : begin + full].reshape(
            whole, depth, lanes
        )
        if half:
            at = pl.ds(pl.multiple_of(place * half, 8), half)
            halves_ref[at] = ref[begin + full : begin + full + half]
    select = pair_selector(slots_ref)
    across = lane_index(depth) % EY
    line = SIDE + 1
    copies, done = [], 0
    for c, first, count in middle_groups(layout, depth, upper):
        put = functools.partial(put_node, nodes_ref, depth)
        end = t_ref[ENDS + c]
        for i in range(first, first + count):
            for j in range(SIDE):
                row = c * INNER + SIDE * (i - 1) + j
                value = u_ref[row]
                if row - base < rows_ref.shape[0]:
                    value += rows_ref[row - base]
                else:
                    value += double(halves_ref, 2 * (row - base - rows_ref.shape[0]), depth)
                at = line * (done + i - first)
                put(at + j, value)
                if j == 0:
                    last = jnp.where(across == EY - 1, roll(end, EY - 1 - i), roll(value, -1))
                    put(at + SIDE, last)
        nodes = nodes_ref[pl.ds(line * done * depth, line * count * depth), :]
        part = pl.ds(line * done, line * count)
        slots_out_ref[part] = to_slots(nodes, select).reshape(line * count, depth, lanes)
        copy = pltpu.make_async_copy(
            slots_out_ref.at[part],
            out_ref.at[c, pl.ds(line * first, line * count)],
            sems.at[len(copies)],
        )
        copy.start()
        copies.append(copy)
        done += count
    for copy in copies:
        copy.wait()


def middle(layout, upper, args, values, result):
    depth = args[0].shape[1]
    sizes = layout.share(depth)
    groups = middle_groups(layout, depth, upper)
    count = (SIDE + 1) * sum(group[2] for group in groups)
    blocks = len(layout.blocks)
    full, half = sizes[2:] if upper else (sizes[0], 0)
    scratch = [
        pltpu.VMEM((count * depth, 2 * LANES), bf16),
        pltpu.VMEM((count, depth, LANES), f32),
        pltpu.SemaphoreType.DMA((len(groups),)),
        pltpu.VMEM((blocks * full // depth, depth, LANES), f32),
        pltpu.VMEM((blocks * max(half, 8), LANES), f32),
    ]
    kernel = functools.partial(middle_kernel, layout, upper)
    return expand(kernel, "upper" if upper else "lower", scratch, (*args, *values), result)


def expand(kernel, name, scratch, args, result=None):
    depth = args[0].shape[1]
    in_specs = [pl.BlockSpec(memory_space=pltpu.VMEM)] * len(args)
    aliases = {}
    if result is not None:
        aliases = {len(args): 0}
        args = (*args, result)
        in_specs.append(pl.BlockSpec(memory_space=pl.ANY))
    return pl.pallas_call(
        kernel,
        in_specs=in_specs,
        out_specs=pl.BlockSpec(memory_space=pl.ANY),
        out_shape=jax.ShapeDtypeStruct((3, NODES, depth, LANES), f32),
        scratch_shapes=scratch,
        input_output_aliases=aliases,
        compiler_params=pltpu.CompilerParams(vmem_limit_bytes=VMEM),
        cost_estimate=pl.CostEstimate(flops=0, bytes_accessed=0, transcendentals=0),
        name=name,
    )(*args)


def beside(faces):
    count = lax.axis_size("dom")
    onward = [(k, (k + 1) % count) for k in range(count)]
    back = [(k, (k - 1) % count) for k in range(count)]
    before = lax.ppermute(faces, "dom", onward)
    return before, before if onward == back else lax.ppermute(faces, "dom", back)


def local(velocity, slot_of_cell, elem_mats, geometry):
    depth = velocity.shape[1]
    layout = Layout(lax.axis_size("modes"))
    args = (velocity.transpose(0, 2, 1, 3), slot_of_cell, elem_mats.transpose(1, 0, 2), geometry)
    table = jnp.asarray(operator(layout, depth))
    early, late = layout.start(*layout.divide(elements("mass", (3,), layout, args)))
    pencil = late + layout.middle(late) + layout.end(early)
    u, u_extras = elements("stiff", (0, 1, 2), None, args)
    table = following([table], u)[0]
    cut = sum(layout.share(depth)[:2])
    early, late = layout.start(*layout.divide(spanwise(layout, depth, pencil, table)))
    lower = layout.middle(late, slice(None, cut))
    upper = layout.middle(late, slice(cut, None))
    ended = layout.end(early)
    total, faces = totals(layout, u_extras, late + lower + ended)
    before, after = beside(faces)
    scratch = [
        pltpu.VMEM((2 * (SIDE + 1) * depth, 2 * LANES), bf16),
        pltpu.VMEM((3, 2, SIDE + 1, depth, LANES), f32),
        pltpu.SemaphoreType.DMA((3, 2)),
    ]
    args = (u, total, slot_of_cell)
    result = middle(layout, False, args, late + lower + ended, None)
    result = expand(faces_kernel, "faces", scratch, (total, before, after, slot_of_cell), result)
    result = middle(layout, True, args, late + upper + ended, result)
    return result.transpose(0, 2, 1, 3)


def solution(mesh):
    in_specs = (P(None, "modes", None, "dom"), P("dom", None), P(), P(None, "dom"))
    out_specs = P(None, "modes", None, "dom")
    return jax.shard_map(local, mesh=mesh, in_specs=in_specs, out_specs=out_specs, check_vma=False)
```

```python
import functools
import math

import jax
import jax.numpy as jnp
import numpy as np
from jax import lax
from jax.experimental import pallas as pl
from jax.experimental.pallas import tpu as pltpu
from jax.sharding import PartitionSpec as P

EX = 16
EY = 8
LANES = EX * EY
NODES = 81
SIDE = 8
INNER = SIDE * (SIDE - 1)
FACE = SIDE * EY
HALF = LANES // 2
ENDS = 3 * SIDE
FACES = ENDS + 3
EXTRAS = FACES + 3
CORNERS = 2 * FACES + 3
HALVES = CORNERS + 1
DEEP = 96
PITCH = 104
TALL = 88
VMEM = 48 * 1024 * 1024
WIDE = 60 * 1024 * 1024

f32 = jnp.float32
bf16 = jnp.bfloat16


def split(values):
    high = values.astype(bf16)
    return high, (values - high.astype(f32)).astype(bf16)


class Layout:

    def __init__(self, parts):
        self.outer = max(d for d in range(1, math.isqrt(parts) + 1) if parts % d == 0)
        self.inner = parts // self.outer
        assert self.inner & (self.inner - 1) == 0
        self.late = [0, self.outer // 2]
        self.early = [k for k in range(1, self.outer) if k not in self.late]
        self.blocks = [(k, s) for k in range(self.outer) for s in range(self.inner)]

    def place(self, k, s):
        me = lax.axis_index("modes")
        out = lax.rem(me // self.inner + (k + self.outer), self.outer)
        return out * self.inner + jnp.bitwise_xor(lax.rem(me, self.inner), s)

    def sent(self, k, s, early, late):
        if k in self.late:
            return late[s].at[self.late.index(k)]
        return early[self.early.index(k)].at[s]

    def share(self, depth):
        count = len(self.blocks)
        full = 3 * INNER // count
        rest = -(-2 * (3 * INNER - full * count) // count)
        if rest == 2:
            full, rest = full + 1, 0
        lower = full // 2
        extra = -(-HALVES // count)
        return lower * depth, extra * depth // 2, (full - lower) * depth, rest * depth // 2

    def base(self, depth):
        return self.share(depth)[0] // depth * len(self.blocks)

    def shapes(self, share):
        early = [(self.inner,) + share] * len(self.early)
        return early + [(len(self.late),) + share] * self.inner

    def divide(self, arrays):
        return arrays[: len(self.early)], arrays[len(self.early) :]

    def got(self, refs):
        inner = self.inner
        late, middle, early = refs[:inner], refs[inner:], refs[inner + len(self.late) - 1 :]
        found = {(0, s): late[s].at[0] for s in range(inner)}
        for at, k in enumerate(self.late[1:]):
            found.update({(k, s): middle[at].at[s] for s in range(inner)})
        for at, k in enumerate(self.early):
            found.update({(k, s): early[s].at[at] for s in range(inner)})
        return found

    def onward(self, value, k):
        parts = self.outer * self.inner
        steps = [(d, (d + k * self.inner) % parts) for d in range(parts)]
        return lax.ppermute(value, "modes", steps)

    def across(self, values):
        pairs = lambda s: [(d, d ^ s) for d in range(self.outer * self.inner)]
        return values[:1] + [
            lax.ppermute(value, "modes", pairs(s)) for s, value in enumerate(values) if s
        ]

    def start(self, early, late):
        early = [self.onward(value, k) for k, value in zip(self.early, early)]
        return early, self.across(list(late))

    def middle(self, late, part=slice(None)):
        return [
            self.onward(jnp.stack([value[at, part] for value in late]), k)
            for at, k in enumerate(self.late)
            if k
        ]

    def end(self, early):
        return self.across([jnp.stack([value[s] for value in early]) for s in range(self.inner)])


def following(values, *earlier):
    return [lax.optimization_barrier((value, *earlier))[0] for value in values]


def operator(layout, depth):
    outer, inner = layout.outer, layout.inner
    length = outer * inner * depth
    half = length // 2
    waves = np.arange(half + 1)
    weights = np.where((waves == 0) | (waves == half), 1.0, 2.0) / length
    sigma = 1.0 + (8.0 * waves / length) ** 2
    phases = (np.arange(length)[:, None] * waves[None, :]) % length
    row = (np.cos(phases * (2.0 * np.pi / length)) * (weights * sigma)).sum(1)
    step, slot, plane = np.meshgrid(np.arange(outer), np.arange(inner), np.arange(depth), indexing="ij")
    step, slot, plane = step.ravel(), slot.ravel(), plane.ravel()
    place = np.arange(inner)[:, None]
    sent = (step * inner + (place ^ slot)) * depth + plane
    got = (-step * inner + (place ^ slot)) * depth + plane
    full = row[(sent[:, :, None] - got[:, None, :]) % length].astype(np.float32)
    high = full.astype(jnp.bfloat16)
    low = (full - high.astype(np.float32)).astype(jnp.bfloat16)
    return np.concatenate([high, low], axis=1)


def selector(slots):
    slot = lax.broadcasted_iota(jnp.int32, (LANES, LANES), 0)
    return jnp.where(slot == slots, 1.0, 0.0).astype(f32)


def lane_index(depth):
    return lax.broadcasted_iota(jnp.int32, (depth, LANES), 1)


def roll(value, shift):
    shift = shift % LANES
    return value if shift == 0 else pltpu.roll(value, shift, 1)


def gather_face(column, origin):
    lane = lane_index(column[0].shape[0])
    face = jnp.where(lane == FACE, roll(column[SIDE], FACE - origin - EY + 1), 0.0)
    for j in range(SIDE):
        face = jnp.where(lane // EY == j, roll(column[j], EY * j - origin), face)
    return face


def prepare(terms, slots_ref, mats_ref, left_ref):
    select = selector(slots_ref[...]).astype(bf16)
    left_ref[...] = jnp.zeros_like(left_ref)
    for place, term in enumerate(terms):
        high, low = split(mats_ref[:, term, :])
        left_ref[place, :NODES, 0:NODES] = high
        left_ref[place, :NODES, NODES : NODES + 1] = low[:, NODES - 1 :]
        left_ref[place, :NODES, TALL : TALL + NODES] = high
        left_ref[place, :NODES, 2 * TALL :] = low[:, : NODES - 1]
    return jnp.concatenate([select, select], axis=0)


def component(terms, first, second, select, geo, left, scratch, row, ends, face):
    values_ref, images_ref, cells_ref = scratch
    depth = first.shape[1]
    values_ref[:NODES, :depth] = first[...] * second[...]
    values_ref[NODES, :depth] = values_ref[NODES - 1, :depth]
    flat = values_ref.reshape(TALL * (depth + 8), LANES)
    for pair in range(0, depth, 2):
        right = []
        for p in (pair, pair + 1):
            value = flat[pl.ds(p, TALL, stride=depth + 8), :]
            high = value.astype(bf16).astype(f32)
            parts = jnp.concatenate([high, value - high, high[: NODES - 1]], axis=0)
            right.append(parts.astype(bf16))
        images = jnp.dot(left, jnp.concatenate(right, axis=1), preferred_element_type=f32)
        for p in (0, 1):
            total = 0.0
            for t, term in enumerate(terms):
                total = total + (
                    images[DEEP * t : DEEP * t + DEEP, LANES * p : LANES * p + LANES]
                    * geo[term : term + 1]
                )
            high, low = split(total)
            images_ref[(pair + p) * DEEP : (pair + p + 1) * DEEP, :LANES] = high
            images_ref[(pair + p) * DEEP : (pair + p + 1) * DEEP, LANES:] = low
    cells = jnp.dot(images_ref[...], select, preferred_element_type=f32)
    for p in range(depth):
        cells_ref[p * PITCH : p * PITCH + DEEP] = cells[p * DEEP : (p + 1) * DEEP]
    lane = lane_index(depth)
    across = lane % EY

    def node(i, j):
        value = cells_ref[pl.ds((SIDE + 1) * i + j, depth, stride=PITCH), :]
        if i > 0:
            return value
        return value + jnp.where(lane >= EY, roll(node(8, j), EY), 0.0)

    def join(low, high):
        return low + jnp.where(across > 0, roll(high, 1), 0.0)

    end = jnp.zeros((depth, LANES), f32)
    for i in range(SIDE + 1):
        column = [node(i, j) for j in range(SIDE + 1)]
        column[0] = join(column[0], column[SIDE])
        if i < SIDE:
            for j in range(SIDE):
                row(SIDE * (i - 1) + j if i else INNER + j, column[j])
            end = jnp.where(across == i, roll(column[SIDE], i + 1 - EY), end)
    ends(end)
    face(gather_face(column, LANES - EY))


def pack(value, half):
    lane = lane_index(value.shape[0] // 2)
    top, bottom = value[: value.shape[0] // 2], value[value.shape[0] // 2 :]
    if half:
        return jnp.where(lane < HALF, roll(top, HALF), bottom)
    return jnp.where(lane < HALF, top, roll(bottom, HALF))


def unpack(packed):
    return jnp.concatenate([packed, roll(packed, HALF)], axis=0)


def element_kernel(terms, layout, count, *refs):
    vel_hbm, slots_hbm, mats_hbm, geo_hbm = refs[:4]
    outs, scratch = refs[4 : 4 + count], refs[4 + count :]
    vel_ref, slots_ref, mats_ref, geo_ref, left_ref, *parts, sems = scratch[:9]
    pairs = [(slots_hbm, slots_ref), (geo_hbm, geo_ref), (mats_hbm, mats_ref)]
    pairs += [(vel_hbm.at[c], vel_ref.at[c]) for c in range(3)]
    copies = [pltpu.make_async_copy(*pair, sems.at[k]) for k, pair in enumerate(pairs)]
    for copy in copies:
        copy.start()
    depth = vel_ref.shape[2]
    parts[0][NODES:] = jnp.zeros((TALL - NODES, depth + 8, LANES), f32)
    sends = []
    corners = [jnp.zeros((depth, LANES), f32)]
    if layout:
        blocks_ref, send_sems = scratch[9:]
        early, late = layout.divide(outs)
        sizes, base = layout.share(depth), layout.base(depth)
        total, lower = sum(sizes), sizes[0]
        full = base + sizes[2] // depth * len(layout.blocks)
        for k, s in layout.blocks:
            place, target = layout.place(k, s), layout.sent(k, s, early, late)
            for begin, end in ((0, lower), (lower, total)):
                source = pl.ds(pl.multiple_of(place * total + begin, 8), end - begin)
                copy = pltpu.make_async_copy(
                    blocks_ref.at[source], target.at[begin:end], send_sems.at[len(sends)]
                )
                sends.append((place, copy))

    def put_block(kind, at, value):
        size = value.shape[0]
        count = sizes[kind] // size
        begin = at // count * total + sum(sizes[:kind]) + at % count * size
        blocks_ref[begin : begin + size] = value

    def put_half(kind, at, value, half=0):
        put_block(kind, at, pack(value, half))

    def put_extra(row, value):
        if layout:
            put_half(1, 2 * row, value)
            put_half(1, 2 * row + 1, value, 1)
        else:
            outs[1][row] = value

    def put_row(c, row, value):
        if row >= INNER:
            put_extra(SIDE * c + row - INNER, value)
            return
        row += c * INNER
        if not layout:
            outs[0][row] = value
        elif row < base:
            put_block(0, row, value)
        elif row < full:
            put_block(2, row - base, value)
        else:
            put_half(3, 2 * (row - full), value)
            put_half(3, 2 * (row - full) + 1, value, 1)

    def put_end(c, value):
        put_extra(ENDS + c, value)

    def put_face(c, value):
        if layout:
            put_half(1, 2 * FACES + c, value)
            corners[0] = jnp.where(lane_index(depth) == c, roll(value, c - FACE), corners[0])
        else:
            outs[1][FACES + c] = value

    for copy in copies[:3]:
        copy.wait()
    select = prepare(terms, slots_ref, mats_ref, left_ref)
    left = left_ref[...].reshape(len(terms) * DEEP, 2 * LANES)
    geo = geo_ref[...]
    copies[3].wait()
    for c in range(3):
        if c < 2:
            copies[4 + c].wait()
        puts = [functools.partial(store, c) for store in (put_row, put_end, put_face)]
        first, second = vel_ref.at[c], vel_ref.at[(c + 1) % 3]
        component(terms, first, second, select, geo, left, parts, *puts)
        for place, copy in sends[::2]:
            count = lower // depth
            before, ready = (min(len(layout.blocks), k * INNER // count) for k in (c, c + 1))
            if before < ready:
                pl.when(jnp.logical_and(place >= before, place < ready))(copy.start)
    if layout:
        put_half(1, CORNERS, corners[0])
        blank = jnp.zeros((depth, LANES), f32)
        for at in range(HALVES, sizes[1] * 2 // depth * len(layout.blocks)):
            put_half(1, at, blank)
        for at in range(3 * INNER - base, full - base):
            put_block(2, at, blank)
        for at in range(2 * max(3 * INNER - full, 0), sizes[3] * 2 // depth * len(layout.blocks)):
            put_half(3, at, blank)
        for _, copy in sends[1::2]:
            copy.start()
        for _, copy in sends:
            copy.wait()


def elements(name, terms, layout, args):
    depth = args[0].shape[2]
    scratch = [
        *(pltpu.VMEM(a.shape, a.dtype) for a in args),
        pltpu.VMEM((len(terms), DEEP, 2 * LANES), bf16),
        pltpu.VMEM((TALL, depth + 8, LANES), f32),
        pltpu.VMEM((DEEP * depth, 2 * LANES), bf16),
        pltpu.VMEM((PITCH * depth, LANES), f32),
        pltpu.SemaphoreType.DMA((6,)),
    ]
    anywhere, vmem = pl.BlockSpec(memory_space=pl.ANY), pl.BlockSpec(memory_space=pltpu.VMEM)
    shapes, specs = [(3 * INNER, depth, LANES)], [vmem]
    if layout:
        count = len(layout.blocks)
        sizes = layout.share(depth)
        scratch.append(pltpu.VMEM((count * sum(sizes), LANES), f32))
        scratch.append(pltpu.SemaphoreType.DMA((2 * count,)))
        shapes = layout.shapes((sum(sizes), LANES))
        specs = [anywhere] * len(shapes)
    else:
        shapes.append((EXTRAS, depth, LANES))
        specs.append(vmem)
    return pl.pallas_call(
        functools.partial(element_kernel, terms, layout, len(shapes)),
        in_specs=[anywhere] * len(args),
        out_specs=specs,
        out_shape=[jax.ShapeDtypeStruct(shape, f32) for shape in shapes],
        scratch_shapes=scratch,
        compiler_params=pltpu.CompilerParams(vmem_limit_bytes=WIDE if layout else VMEM),
        cost_estimate=pl.CostEstimate(
            flops=2 * 3 * depth * len(terms) * DEEP * 3 * DEEP * LANES,
            bytes_accessed=4 * 3 * depth * LANES * 150,
            transcendentals=0,
        ),
        name=name,
    )(*args)


def left_sums(before, j):
    lane = lane_index(before.shape[0])
    if j < SIDE:
        return jnp.where(lane < EY, roll(before, -EY * j), 0.0)
    return jnp.where(lane == 0, roll(before, -FACE), 0.0)


def spanwise_kernel(layout, depth, count, *refs):
    got = layout.got(refs[:count])
    table_ref, early, late = refs[count], *layout.divide(refs[count + 1 :])
    length = len(layout.blocks) * depth
    table = table_ref[lax.rem(lax.axis_index("modes"), layout.inner)]
    rows, begin = [], 0
    for sublanes, size in zip(layout.share(depth), (depth, depth // 2) * 2):
        rows += [(at, size) for at in range(begin, begin + sublanes, size)]
        begin += sublanes
    for first in range(0, len(rows), 2):
        group = rows[first : first + 2]
        x = []
        for at, size in group:
            blocks = [got[block][at : at + size] for block in layout.blocks]
            if size < depth:
                blocks = [unpack(block) for block in blocks]
            x.append(jnp.concatenate(blocks, axis=0))
        x_high, x_low = split(jnp.concatenate(x, axis=1))
        y = jnp.dot(table, x_high, preferred_element_type=f32)
        y = y[:length] + y[length:]
        y += jnp.dot(table[:length], x_low, preferred_element_type=f32)
        for place, block in enumerate(layout.blocks):
            for k, (at, size) in enumerate(group):
                value = y[depth * place : depth * place + depth, LANES * k : LANES * k + LANES]
                value = value if size == depth else pack(value, 0)
                layout.sent(*block, early, late)[at : at + size] = value


def spanwise(layout, depth, values, table):
    length = len(layout.blocks) * depth
    sizes = layout.share(depth)
    shapes = layout.shapes((sum(sizes), LANES))
    return pl.pallas_call(
        functools.partial(spanwise_kernel, layout, depth, len(values)),
        out_shape=[jax.ShapeDtypeStruct(shape, f32) for shape in shapes],
        compiler_params=pltpu.CompilerParams(vmem_limit_bytes=VMEM),
        cost_estimate=pl.CostEstimate(
            flops=6 * length * len(layout.blocks) * sum(sizes) * LANES,
            bytes_accessed=8 * len(layout.blocks) * sum(sizes) * LANES,
            transcendentals=0,
        ),
        name="spanwise",
    )(*values, table)


def to_slots(nodes, select):
    return lax.dot_general(nodes, select, (((1,), (1,)), ((), ())), preferred_element_type=f32)


def pair_selector(slots_ref):
    select = selector(slots_ref[...]).astype(bf16)
    return jnp.concatenate([select, select], axis=1)


def single(ref, at, depth):
    return unpack(ref[at * depth // 2 : (at + 1) * depth // 2])


def double(ref, at, depth):
    lower, upper = single(ref, at, depth), single(ref, at + 1, depth)
    return jnp.where(lane_index(depth) < HALF, lower, roll(upper, HALF))


def totals_kernel(layout, u_ref, *refs):
    total_ref, faces_ref, halves_ref = refs[-3:]
    depth = u_ref.shape[1]
    begin, size = layout.share(depth)[:2]
    for (k, s), ref in layout.got(refs[:-3]).items():
        at = pl.ds(pl.multiple_of(layout.place(-k, s) * size, 8), size)
        halves_ref[at] = ref[begin : begin + size]
    corners = single(halves_ref, CORNERS, depth)
    lane = lane_index(depth)
    last = jnp.zeros((depth, LANES), f32)
    for c in range(3):
        column = []
        for j in range(SIDE + 1):
            row = ENDS + c if j == SIDE else SIDE * c + j
            column.append(u_ref[row] + double(halves_ref, 2 * row, depth))
            total_ref[row] = column[j]
        face = single(halves_ref, 2 * FACES + c, depth)
        face = jnp.where(lane_index(depth) == FACE, roll(corners, FACE - c), face)
        face += u_ref[FACES + c]
        total_ref[FACES + c] = face
        left = gather_face(column[:SIDE] + [roll(column[SIDE], EY - 1)], 0)
        faces_ref[c] = jnp.where(lane < HALF, face, roll(left, HALF))
        last = jnp.where(lane == c, roll(face, c - FACE), last)
        last = jnp.where(lane == SIDE + c, roll(left, SIDE + c - FACE), last)
    faces_ref[3] = last


def totals(layout, u, values):
    depth = u.shape[1]
    size = layout.share(depth)[1]
    return pl.pallas_call(
        functools.partial(totals_kernel, layout),
        out_shape=[
            jax.ShapeDtypeStruct(u.shape, f32),
            jax.ShapeDtypeStruct((4, depth, LANES), f32),
        ],
        scratch_shapes=[pltpu.VMEM((len(layout.blocks) * size, LANES), f32)],
        compiler_params=pltpu.CompilerParams(vmem_limit_bytes=VMEM),
        cost_estimate=pl.CostEstimate(flops=0, bytes_accessed=0, transcendentals=0),
        name="totals",
    )(u, *values)


def put_node(nodes_ref, depth, at, value):
    high, low = split(value)
    nodes_ref[pl.ds(at * depth, depth), :] = jnp.concatenate([high, low], axis=1)


def faces_nodes(t_ref, before_ref, after_ref, select, out_ref, nodes_ref, slots_out_ref, sems):
    depth, lanes = t_ref.shape[1:]
    lane = lane_index(depth)
    across = lane % EY
    count = SIDE + 1
    copies = []
    for c in range(3):
        put = functools.partial(put_node, nodes_ref, depth)
        before = jnp.where(lane == FACE, roll(before_ref[3], FACE - c), before_ref[c])
        after = roll(after_ref[c], HALF)
        after = jnp.where(lane == FACE, roll(after_ref[3], FACE - SIDE - c), after)
        face = t_ref[FACES + c] + after
        end = t_ref[ENDS + c] + left_sums(before, SIDE)
        for j in range(SIDE):
            value = t_ref[SIDE * c + j] + left_sums(before, j)
            moved = roll(face, lanes - EY - EY * j)
            beyond = jnp.where(lane >= lanes - EY, moved, roll(value, -EY))
            put(j, value)
            put(count + j, beyond)
            if j == 0:
                last = jnp.where(across == EY - 1, roll(end, EY - 1), roll(value, -1))
                put(SIDE, last)
                corner = jnp.where(across == EY - 1, roll(end, -1), roll(beyond, -1))
                corner = jnp.where(lane == lanes - 1, roll(face, lanes - 1 - FACE), corner)
                put(count + SIDE, corner)
        slots_out_ref[c] = to_slots(nodes_ref[...], select).reshape(2, count, depth, lanes)
        for side in range(2):
            copy = pltpu.make_async_copy(
                slots_out_ref.at[c, side],
                out_ref.at[c, pl.ds(side * (NODES - count), count)],
                sems.at[c, side],
            )
            copy.start()
            copies.append(copy)
    return copies


def middle_groups(layout, depth, upper):
    group = SIDE - 1
    cut = layout.base(depth) // SIDE
    first, last = (cut, 3 * group) if upper else (0, cut)
    groups = []
    while first < last:
        count = min(last - first, group - first % group)
        groups.append((first // group, first % group + 1, count))
        first += count
    return groups


def middle_nodes(layout, upper, u_ref, t_ref, select, values, out_ref, scratch):
    nodes_ref, slots_out_ref, sems, rows_ref, halves_ref = scratch
    depth, lanes = u_ref.shape[1:]
    sizes = layout.share(depth)
    full, half = sizes[2:] if upper else (sizes[0], 0)
    base = layout.base(depth) if upper else 0
    whole = full // depth
    for (k, s), ref in layout.got(values).items():
        place = layout.place(-k, s)
        begin = sum(sizes[:2]) if upper and k != layout.late[1] else 0
        rows_ref[pl.ds(place * whole, whole)] = ref[begin : begin + full].reshape(
            whole, depth, lanes
        )
        if half:
            at = pl.ds(pl.multiple_of(place * half, 8), half)
            halves_ref[at] = ref[begin + full : begin + full + half]
    across = lane_index(depth) % EY
    line = SIDE + 1
    copies, done = [], 0
    for c, first, count in middle_groups(layout, depth, upper):
        put = functools.partial(put_node, nodes_ref, depth)
        end = t_ref[ENDS + c]
        for i in range(first, first + count):
            for j in range(SIDE):
                row = c * INNER + SIDE * (i - 1) + j
                value = u_ref[row]
                if row - base < rows_ref.shape[0]:
                    value += rows_ref[row - base]
                else:
                    value += double(halves_ref, 2 * (row - base - rows_ref.shape[0]), depth)
                at = line * (done + i - first)
                put(at + j, value)
                if j == 0:
                    last = jnp.where(across == EY - 1, roll(end, EY - 1 - i), roll(value, -1))
                    put(at + SIDE, last)
        nodes = nodes_ref[pl.ds(line * done * depth, line * count * depth), :]
        part = pl.ds(line * done, line * count)
        slots_out_ref[part] = to_slots(nodes, select).reshape(line * count, depth, lanes)
        copy = pltpu.make_async_copy(
            slots_out_ref.at[part],
            out_ref.at[c, pl.ds(line * first, line * count)],
            sems.at[len(copies)],
        )
        copy.start()
        copies.append(copy)
        done += count
    return copies


def lower_kernel(layout, u_ref, t_ref, slots_ref, *refs):
    values, out_ref, scratch = refs[:-6], refs[-6], refs[-5:]
    select = pair_selector(slots_ref)
    for copy in middle_nodes(layout, False, u_ref, t_ref, select, values, out_ref, scratch):
        copy.wait()


def upper_kernel(layout, u_ref, t_ref, slots_ref, before_ref, after_ref, *refs):
    values, out_ref, scratch = refs[:-10], refs[-9], refs[-8:]
    select = pair_selector(slots_ref)
    copies = middle_nodes(layout, True, u_ref, t_ref, select, values, out_ref, scratch[:5])
    copies += faces_nodes(t_ref, before_ref, after_ref, select, out_ref, *scratch[5:])
    for copy in copies:
        copy.wait()


def middle_scratch(layout, depth, upper):
    sizes = layout.share(depth)
    groups = middle_groups(layout, depth, upper)
    count = (SIDE + 1) * sum(group[2] for group in groups)
    blocks = len(layout.blocks)
    full, half = sizes[2:] if upper else (sizes[0], 0)
    return [
        pltpu.VMEM((count * depth, 2 * LANES), bf16),
        pltpu.VMEM((count, depth, LANES), f32),
        pltpu.SemaphoreType.DMA((len(groups),)),
        pltpu.VMEM((blocks * full // depth, depth, LANES), f32),
        pltpu.VMEM((blocks * max(half, 8), LANES), f32),
    ]


def expand(kernel, name, scratch, args, result=None):
    depth = args[0].shape[1]
    in_specs = [pl.BlockSpec(memory_space=pltpu.VMEM)] * len(args)
    aliases = {}
    if result is not None:
        aliases = {len(args): 0}
        args = (*args, result)
        in_specs.append(pl.BlockSpec(memory_space=pl.ANY))
    return pl.pallas_call(
        kernel,
        in_specs=in_specs,
        out_specs=pl.BlockSpec(memory_space=pl.ANY),
        out_shape=jax.ShapeDtypeStruct((3, NODES, depth, LANES), f32),
        scratch_shapes=scratch,
        input_output_aliases=aliases,
        compiler_params=pltpu.CompilerParams(vmem_limit_bytes=VMEM),
        cost_estimate=pl.CostEstimate(flops=0, bytes_accessed=0, transcendentals=0),
        name=name,
    )(*args)


def beside(faces):
    count = lax.axis_size("dom")
    onward = [(k, (k + 1) % count) for k in range(count)]
    back = [(k, (k - 1) % count) for k in range(count)]
    before = lax.ppermute(faces, "dom", onward)
    return before, before if onward == back else lax.ppermute(faces, "dom", back)


def local(velocity, slot_of_cell, elem_mats, geometry):
    depth = velocity.shape[1]
    layout = Layout(lax.axis_size("modes"))
    args = (velocity.transpose(0, 2, 1, 3), slot_of_cell, elem_mats.transpose(1, 0, 2), geometry)
    table = jnp.asarray(operator(layout, depth))
    early, late = layout.start(*layout.divide(elements("mass", (3,), layout, args)))
    pencil = late + layout.middle(late) + layout.end(early)
    u, u_extras = elements("stiff", (0, 1, 2), None, args)
    table = following([table], u)[0]
    cut = sum(layout.share(depth)[:2])
    early, late = layout.start(*layout.divide(spanwise(layout, depth, pencil, table)))
    lower = layout.middle(late, slice(None, cut))
    upper = layout.middle(late, slice(cut, None))
    ended = layout.end(early)
    total, faces = totals(layout, u_extras, late + lower + ended)
    before, after = beside(faces)
    scratch = middle_scratch(layout, depth, False)
    args = (u, total, slot_of_cell)
    kernel = functools.partial(lower_kernel, layout)
    result = expand(kernel, "lower", scratch, (*args, *late, *lower, *ended))
    scratch = middle_scratch(layout, depth, True) + [
        pltpu.VMEM((2 * (SIDE + 1) * depth, 2 * LANES), bf16),
        pltpu.VMEM((3, 2, SIDE + 1, depth, LANES), f32),
        pltpu.SemaphoreType.DMA((3, 2)),
    ]
    kernel = functools.partial(upper_kernel, layout)
    args += (before, after, *late, *upper, *ended)
    result = expand(kernel, "upper", scratch, args, result)
    return result.transpose(0, 2, 1, 3)


def solution(mesh):
    in_specs = (P(None, "modes", None, "dom"), P("dom", None), P(), P(None, "dom"))
    out_specs = P(None, "modes", None, "dom")
    return jax.shard_map(local, mesh=mesh, in_specs=in_specs, out_specs=out_specs, check_vma=False)
```

```python
import functools
import math

import jax
import jax.numpy as jnp
import numpy as np
from jax import lax
from jax.experimental import pallas as pl
from jax.experimental.pallas import tpu as pltpu
from jax.sharding import PartitionSpec as P

EX = 16
EY = 8
LANES = EX * EY
NODES = 81
SIDE = 8
INNER = SIDE * (SIDE - 1)
FACE = SIDE * EY
HALF = LANES // 2
ENDS = 3 * SIDE
FACES = ENDS + 3
EXTRAS = FACES + 3
CORNERS = 2 * FACES + 3
HALVES = CORNERS + 1
DEEP = 96
PITCH = 104
TALL = 88
VMEM = 48 * 1024 * 1024
WIDE = 60 * 1024 * 1024

f32 = jnp.float32
bf16 = jnp.bfloat16


def split(values):
    high = values.astype(bf16)
    return high, (values - high.astype(f32)).astype(bf16)


class Layout:

    def __init__(self, parts):
        self.outer = max(d for d in range(1, math.isqrt(parts) + 1) if parts % d == 0)
        self.inner = parts // self.outer
        assert self.inner & (self.inner - 1) == 0
        self.late = [0, self.outer // 2]
        self.early = [k for k in range(1, self.outer) if k not in self.late]
        self.blocks = [(k, s) for k in range(self.outer) for s in range(self.inner)]

    def place(self, k, s):
        me = lax.axis_index("modes")
        out = lax.rem(me // self.inner + (k + self.outer), self.outer)
        return out * self.inner + jnp.bitwise_xor(lax.rem(me, self.inner), s)

    def sent(self, k, s, early, late):
        if k in self.late:
            return late[s].at[self.late.index(k)]
        return early[self.early.index(k)].at[s]

    def share(self, depth):
        count = len(self.blocks)
        full = 3 * INNER // count
        rest = -(-2 * (3 * INNER - full * count) // count)
        if rest == 2:
            full, rest = full + 1, 0
        lower = full // 2
        extra = -(-HALVES // count)
        return lower * depth, extra * depth // 2, (full - lower) * depth, rest * depth // 2

    def base(self, depth):
        return self.share(depth)[0] // depth * len(self.blocks)

    def shapes(self, share):
        early = [(self.inner,) + share] * len(self.early)
        return early + [(len(self.late),) + share] * self.inner

    def divide(self, arrays):
        return arrays[: len(self.early)], arrays[len(self.early) :]

    def got(self, refs):
        inner = self.inner
        late, middle, early = refs[:inner], refs[inner:], refs[inner + len(self.late) - 1 :]
        found = {(0, s): late[s].at[0] for s in range(inner)}
        for at, k in enumerate(self.late[1:]):
            found.update({(k, s): middle[at].at[s] for s in range(inner)})
        for at, k in enumerate(self.early):
            found.update({(k, s): early[s].at[at] for s in range(inner)})
        return found

    def onward(self, value, k):
        parts = self.outer * self.inner
        steps = [(d, (d + k * self.inner) % parts) for d in range(parts)]
        return lax.ppermute(value, "modes", steps)

    def across(self, values):
        pairs = lambda s: [(d, d ^ s) for d in range(self.outer * self.inner)]
        return values[:1] + [
            lax.ppermute(value, "modes", pairs(s)) for s, value in enumerate(values) if s
        ]

    def start(self, early, late):
        early = [self.onward(value, k) for k, value in zip(self.early, early)]
        return early, self.across(list(late))

    def middle(self, late, part=slice(None)):
        return [
            self.onward(jnp.stack([value[at, part] for value in late]), k)
            for at, k in enumerate(self.late)
            if k
        ]

    def end(self, early):
        return self.across([jnp.stack([value[s] for value in early]) for s in range(self.inner)])


def following(values, *earlier):
    return [lax.optimization_barrier((value, *earlier))[0] for value in values]


def operator(layout, depth):
    outer, inner = layout.outer, layout.inner
    length = outer * inner * depth
    half = length // 2
    waves = np.arange(half + 1)
    weights = np.where((waves == 0) | (waves == half), 1.0, 2.0) / length
    sigma = 1.0 + (8.0 * waves / length) ** 2
    phases = (np.arange(length)[:, None] * waves[None, :]) % length
    row = (np.cos(phases * (2.0 * np.pi / length)) * (weights * sigma)).sum(1)
    step, slot, plane = np.meshgrid(np.arange(outer), np.arange(inner), np.arange(depth), indexing="ij")
    step, slot, plane = step.ravel(), slot.ravel(), plane.ravel()
    place = np.arange(inner)[:, None]
    sent = (step * inner + (place ^ slot)) * depth + plane
    got = (-step * inner + (place ^ slot)) * depth + plane
    full = row[(sent[:, :, None] - got[:, None, :]) % length].astype(np.float32)
    high = full.astype(jnp.bfloat16)
    low = (full - high.astype(np.float32)).astype(jnp.bfloat16)
    return np.concatenate([high, low], axis=1)


def selector(slots):
    slot = lax.broadcasted_iota(jnp.int32, (LANES, LANES), 0)
    return jnp.where(slot == slots, 1.0, 0.0).astype(f32)


def lane_index(depth):
    return lax.broadcasted_iota(jnp.int32, (depth, LANES), 1)


def roll(value, shift):
    shift = shift % LANES
    return value if shift == 0 else pltpu.roll(value, shift, 1)


def gather_face(column, origin):
    lane = lane_index(column[0].shape[0])
    face = jnp.where(lane == FACE, roll(column[SIDE], FACE - origin - EY + 1), 0.0)
    for j in range(SIDE):
        face = jnp.where(lane // EY == j, roll(column[j], EY * j - origin), face)
    return face


def prepare(terms, slots_ref, mats_ref, left_ref):
    select = selector(slots_ref[...]).astype(bf16)
    left_ref[...] = jnp.zeros_like(left_ref)
    for place, term in enumerate(terms):
        high, low = split(mats_ref[:, term, :])
        left_ref[place, :NODES, 0:NODES] = high
        left_ref[place, :NODES, NODES : NODES + 1] = low[:, NODES - 1 :]
        left_ref[place, :NODES, TALL : TALL + NODES] = high
        left_ref[place, :NODES, 2 * TALL :] = low[:, : NODES - 1]
    return jnp.concatenate([select, select], axis=0)


def component(terms, first, second, select, geo, left, scratch, row, ends, face):
    values_ref, images_ref, cells_ref = scratch
    depth = first.shape[1]
    values_ref[:NODES, :depth] = first[...] * second[...]
    values_ref[NODES, :depth] = values_ref[NODES - 1, :depth]
    flat = values_ref.reshape((TALL + 1) * (depth + 8), LANES)
    for pair in range(0, depth, 2):
        right = []
        for p in (pair, pair + 1):
            value = flat[pl.ds(p, TALL, stride=depth + 8), :]
            high = value.astype(bf16).astype(f32)
            parts = jnp.concatenate([high, value - high, high[: NODES - 1]], axis=0)
            right.append(parts.astype(bf16))
        images = jnp.dot(left, jnp.concatenate(right, axis=1), preferred_element_type=f32)
        for p in (0, 1):
            total = 0.0
            for t, term in enumerate(terms):
                total = total + (
                    images[DEEP * t : DEEP * t + DEEP, LANES * p : LANES * p + LANES]
                    * geo[term : term + 1]
                )
            high, low = split(total)
            images_ref[(pair + p) * DEEP : (pair + p + 1) * DEEP, :LANES] = high
            images_ref[(pair + p) * DEEP : (pair + p + 1) * DEEP, LANES:] = low
    cells = jnp.dot(images_ref[...], select, preferred_element_type=f32)
    for p in range(depth):
        cells_ref[p * PITCH : p * PITCH + DEEP] = cells[p * DEEP : (p + 1) * DEEP]
    lane = lane_index(depth)
    across = lane % EY

    def node(i, j):
        value = cells_ref[pl.ds((SIDE + 1) * i + j, depth, stride=PITCH), :]
        if i > 0:
            return value
        return value + jnp.where(lane >= EY, roll(node(8, j), EY), 0.0)

    def join(low, high):
        return low + jnp.where(across > 0, roll(high, 1), 0.0)

    end = jnp.zeros((depth, LANES), f32)
    for i in range(SIDE + 1):
        column = [node(i, j) for j in range(SIDE + 1)]
        column[0] = join(column[0], column[SIDE])
        if i < SIDE:
            for j in range(SIDE):
                row(SIDE * (i - 1) + j if i else INNER + j, column[j])
            end = jnp.where(across == i, roll(column[SIDE], i + 1 - EY), end)
    ends(end)
    face(gather_face(column, LANES - EY))


def pack(value, half):
    lane = lane_index(value.shape[0] // 2)
    top, bottom = value[: value.shape[0] // 2], value[value.shape[0] // 2 :]
    if half:
        return jnp.where(lane < HALF, roll(top, HALF), bottom)
    return jnp.where(lane < HALF, top, roll(bottom, HALF))


def unpack(packed):
    return jnp.concatenate([packed, roll(packed, HALF)], axis=0)


def element_kernel(terms, layout, count, *refs):
    vel_hbm, slots_hbm, mats_hbm, geo_hbm = refs[:4]
    outs, scratch = refs[4 : 4 + count], refs[4 + count :]
    vel_ref, slots_ref, mats_ref, geo_ref, left_ref, *parts, sems = scratch[:9]
    pairs = [(slots_hbm, slots_ref), (geo_hbm, geo_ref), (mats_hbm, mats_ref)]
    pairs += [(vel_hbm.at[c], vel_ref.at[c]) for c in range(3)]
    copies = [pltpu.make_async_copy(*pair, sems.at[k]) for k, pair in enumerate(pairs)]
    for copy in copies:
        copy.start()
    depth = vel_ref.shape[2]
    parts[0][NODES:] = jnp.zeros((TALL + 1 - NODES, depth + 8, LANES), f32)
    sends = []
    corners = [jnp.zeros((depth, LANES), f32)]
    if layout:
        blocks_ref, send_sems = scratch[9:]
        early, late = layout.divide(outs)
        sizes, base = layout.share(depth), layout.base(depth)
        total, lower = sum(sizes), sizes[0]
        full = base + sizes[2] // depth * len(layout.blocks)
        for k, s in layout.blocks:
            place, target = layout.place(k, s), layout.sent(k, s, early, late)
            for begin, end in ((0, lower), (lower, total)):
                source = pl.ds(pl.multiple_of(place * total + begin, 8), end - begin)
                copy = pltpu.make_async_copy(
                    blocks_ref.at[source], target.at[begin:end], send_sems.at[len(sends)]
                )
                sends.append((place, copy))

    def put_block(kind, at, value):
        size = value.shape[0]
        count = sizes[kind] // size
        begin = at // count * total + sum(sizes[:kind]) + at % count * size
        blocks_ref[begin : begin + size] = value

    def put_half(kind, at, value, half=0):
        put_block(kind, at, pack(value, half))

    def put_extra(row, value):
        if layout:
            put_half(1, 2 * row, value)
            put_half(1, 2 * row + 1, value, 1)
        else:
            outs[1][row] = value

    def put_row(c, row, value):
        if row >= INNER:
            put_extra(SIDE * c + row - INNER, value)
            return
        row += c * INNER
        if not layout:
            outs[0][row] = value
        elif row < base:
            put_block(0, row, value)
        elif row < full:
            put_block(2, row - base, value)
        else:
            put_half(3, 2 * (row - full), value)
            put_half(3, 2 * (row - full) + 1, value, 1)

    def put_end(c, value):
        put_extra(ENDS + c, value)

    def put_face(c, value):
        if layout:
            put_half(1, 2 * FACES + c, value)
            corners[0] = jnp.where(lane_index(depth) == c, roll(value, c - FACE), corners[0])
        else:
            outs[1][FACES + c] = value

    for copy in copies[:3]:
        copy.wait()
    select = prepare(terms, slots_ref, mats_ref, left_ref)
    left = left_ref[...].reshape(len(terms) * DEEP, 2 * LANES)
    geo = geo_ref[...]
    copies[3].wait()
    for c in range(3):
        if c < 2:
            copies[4 + c].wait()
        puts = [functools.partial(store, c) for store in (put_row, put_end, put_face)]
        first, second = vel_ref.at[c], vel_ref.at[(c + 1) % 3]
        component(terms, first, second, select, geo, left, parts, *puts)
        for place, copy in sends[::2]:
            count = lower // depth
            before, ready = (min(len(layout.blocks), k * INNER // count) for k in (c, c + 1))
            if before < ready:
                pl.when(jnp.logical_and(place >= before, place < ready))(copy.start)
    if layout:
        put_half(1, CORNERS, corners[0])
        blank = jnp.zeros((depth, LANES), f32)
        for at in range(HALVES, sizes[1] * 2 // depth * len(layout.blocks)):
            put_half(1, at, blank)
        for at in range(3 * INNER - base, full - base):
            put_block(2, at, blank)
        for at in range(2 * max(3 * INNER - full, 0), sizes[3] * 2 // depth * len(layout.blocks)):
            put_half(3, at, blank)
        for _, copy in sends[1::2]:
            copy.start()
        for _, copy in sends:
            copy.wait()


def elements(name, terms, layout, args):
    depth = args[0].shape[2]
    scratch = [
        *(pltpu.VMEM(a.shape, a.dtype) for a in args),
        pltpu.VMEM((len(terms), DEEP, 2 * LANES), bf16),
        pltpu.VMEM((TALL + 1, depth + 8, LANES), f32),
        pltpu.VMEM((DEEP * depth, 2 * LANES), bf16),
        pltpu.VMEM((PITCH * (depth + 1), LANES), f32),
        pltpu.SemaphoreType.DMA((6,)),
    ]
    anywhere, vmem = pl.BlockSpec(memory_space=pl.ANY), pl.BlockSpec(memory_space=pltpu.VMEM)
    shapes, specs = [(3 * INNER, depth, LANES)], [vmem]
    if layout:
        count = len(layout.blocks)
        sizes = layout.share(depth)
        scratch.append(pltpu.VMEM((count * sum(sizes), LANES), f32))
        scratch.append(pltpu.SemaphoreType.DMA((2 * count,)))
        shapes = layout.shapes((sum(sizes), LANES))
        specs = [anywhere] * len(shapes)
    else:
        shapes.append((EXTRAS, depth, LANES))
        specs.append(vmem)
    return pl.pallas_call(
        functools.partial(element_kernel, terms, layout, len(shapes)),
        in_specs=[anywhere] * len(args),
        out_specs=specs,
        out_shape=[jax.ShapeDtypeStruct(shape, f32) for shape in shapes],
        scratch_shapes=scratch,
        compiler_params=pltpu.CompilerParams(vmem_limit_bytes=WIDE if layout else VMEM),
        cost_estimate=pl.CostEstimate(
            flops=2 * 3 * depth * len(terms) * DEEP * 3 * DEEP * LANES,
            bytes_accessed=4 * 3 * depth * LANES * 150,
            transcendentals=0,
        ),
        name=name,
    )(*args)


def left_sums(before, j):
    lane = lane_index(before.shape[0])
    if j < SIDE:
        return jnp.where(lane < EY, roll(before, -EY * j), 0.0)
    return jnp.where(lane == 0, roll(before, -FACE), 0.0)


def spanwise_kernel(layout, depth, count, *refs):
    got = layout.got(refs[:count])
    table_ref, early, late = refs[count], *layout.divide(refs[count + 1 :])
    length = len(layout.blocks) * depth
    table = table_ref[lax.rem(lax.axis_index("modes"), layout.inner)]
    rows, begin = [], 0
    for sublanes, size in zip(layout.share(depth), (depth, depth // 2) * 2):
        rows += [(at, size) for at in range(begin, begin + sublanes, size)]
        begin += sublanes
    for first in range(0, len(rows), 2):
        group = rows[first : first + 2]
        x = []
        for at, size in group:
            blocks = [got[block][at : at + size] for block in layout.blocks]
            if size < depth:
                blocks = [unpack(block) for block in blocks]
            x.append(jnp.concatenate(blocks, axis=0))
        x_high, x_low = split(jnp.concatenate(x, axis=1))
        y = jnp.dot(table, x_high, preferred_element_type=f32)
        y = y[:length] + y[length:]
        y += jnp.dot(table[:length], x_low, preferred_element_type=f32)
        for place, block in enumerate(layout.blocks):
            for k, (at, size) in enumerate(group):
                value = y[depth * place : depth * place + depth, LANES * k : LANES * k + LANES]
                value = value if size == depth else pack(value, 0)
                layout.sent(*block, early, late)[at : at + size] = value


def spanwise(layout, depth, values, table):
    length = len(layout.blocks) * depth
    sizes = layout.share(depth)
    shapes = layout.shapes((sum(sizes), LANES))
    return pl.pallas_call(
        functools.partial(spanwise_kernel, layout, depth, len(values)),
        out_shape=[jax.ShapeDtypeStruct(shape, f32) for shape in shapes],
        compiler_params=pltpu.CompilerParams(vmem_limit_bytes=VMEM),
        cost_estimate=pl.CostEstimate(
            flops=6 * length * len(layout.blocks) * sum(sizes) * LANES,
            bytes_accessed=8 * len(layout.blocks) * sum(sizes) * LANES,
            transcendentals=0,
        ),
        name="spanwise",
    )(*values, table)


def to_slots(nodes, select):
    return lax.dot_general(nodes, select, (((1,), (1,)), ((), ())), preferred_element_type=f32)


def pair_selector(slots_ref):
    select = selector(slots_ref[...]).astype(bf16)
    return jnp.concatenate([select, select], axis=1)


def single(ref, at, depth):
    return unpack(ref[at * depth // 2 : (at + 1) * depth // 2])


def double(ref, at, depth):
    lower, upper = single(ref, at, depth), single(ref, at + 1, depth)
    return jnp.where(lane_index(depth) < HALF, lower, roll(upper, HALF))


def totals_kernel(layout, u_ref, *refs):
    total_ref, faces_ref, halves_ref = refs[-3:]
    depth = u_ref.shape[1]
    begin, size = layout.share(depth)[:2]
    for (k, s), ref in layout.got(refs[:-3]).items():
        at = pl.ds(pl.multiple_of(layout.place(-k, s) * size, 8), size)
        halves_ref[at] = ref[begin : begin + size]
    corners = single(halves_ref, CORNERS, depth)
    lane = lane_index(depth)
    last = jnp.zeros((depth, LANES), f32)
    for c in range(3):
        column = []
        for j in range(SIDE + 1):
            row = ENDS + c if j == SIDE else SIDE * c + j
            column.append(u_ref[row] + double(halves_ref, 2 * row, depth))
            total_ref[row] = column[j]
        face = single(halves_ref, 2 * FACES + c, depth)
        face = jnp.where(lane_index(depth) == FACE, roll(corners, FACE - c), face)
        face += u_ref[FACES + c]
        total_ref[FACES + c] = face
        left = gather_face(column[:SIDE] + [roll(column[SIDE], EY - 1)], 0)
        faces_ref[c] = jnp.where(lane < HALF, face, roll(left, HALF))
        last = jnp.where(lane == c, roll(face, c - FACE), last)
        last = jnp.where(lane == SIDE + c, roll(left, SIDE + c - FACE), last)
    faces_ref[3] = last


def totals(layout, u, values):
    depth = u.shape[1]
    size = layout.share(depth)[1]
    return pl.pallas_call(
        functools.partial(totals_kernel, layout),
        out_shape=[
            jax.ShapeDtypeStruct(u.shape, f32),
            jax.ShapeDtypeStruct((4, depth, LANES), f32),
        ],
        scratch_shapes=[pltpu.VMEM((len(layout.blocks) * size, LANES), f32)],
        compiler_params=pltpu.CompilerParams(vmem_limit_bytes=VMEM),
        cost_estimate=pl.CostEstimate(flops=0, bytes_accessed=0, transcendentals=0),
        name="totals",
    )(u, *values)


def put_node(nodes_ref, depth, at, value):
    high, low = split(value)
    nodes_ref[pl.ds(at * depth, depth), :] = jnp.concatenate([high, low], axis=1)


def faces_nodes(t_ref, before_ref, after_ref, select, out_ref, nodes_ref, slots_out_ref, sems):
    depth, lanes = t_ref.shape[1:]
    lane = lane_index(depth)
    across = lane % EY
    count = SIDE + 1
    copies = []
    for c in range(3):
        put = functools.partial(put_node, nodes_ref, depth)
        before = jnp.where(lane == FACE, roll(before_ref[3], FACE - c), before_ref[c])
        after = roll(after_ref[c], HALF)
        after = jnp.where(lane == FACE, roll(after_ref[3], FACE - SIDE - c), after)
        face = t_ref[FACES + c] + after
        end = t_ref[ENDS + c] + left_sums(before, SIDE)
        for j in range(SIDE):
            value = t_ref[SIDE * c + j] + left_sums(before, j)
            moved = roll(face, lanes - EY - EY * j)
            beyond = jnp.where(lane >= lanes - EY, moved, roll(value, -EY))
            put(j, value)
            put(count + j, beyond)
            if j == 0:
                last = jnp.where(across == EY - 1, roll(end, EY - 1), roll(value, -1))
                put(SIDE, last)
                corner = jnp.where(across == EY - 1, roll(end, -1), roll(beyond, -1))
                corner = jnp.where(lane == lanes - 1, roll(face, lanes - 1 - FACE), corner)
                put(count + SIDE, corner)
        slots_out_ref[c] = to_slots(nodes_ref[...], select).reshape(2, count, depth, lanes)
        for side in range(2):
            copy = pltpu.make_async_copy(
                slots_out_ref.at[c, side],
                out_ref.at[c, pl.ds(side * (NODES - count), count)],
                sems.at[c, side],
            )
            copy.start()
            copies.append(copy)
    return copies


def middle_groups(layout, depth, upper):
    group = SIDE - 1
    cut = layout.base(depth) // SIDE
    first, last = (cut, 3 * group) if upper else (0, cut)
    groups = []
    while first < last:
        count = min(last - first, group - first % group)
        groups.append((first // group, first % group + 1, count))
        first += count
    return groups


def middle_nodes(layout, upper, u_ref, t_ref, select, values, out_ref, scratch):
    nodes_ref, slots_out_ref, sems, rows_ref, halves_ref = scratch
    depth, lanes = u_ref.shape[1:]
    sizes = layout.share(depth)
    full, half = sizes[2:] if upper else (sizes[0], 0)
    base = layout.base(depth) if upper else 0
    whole = full // depth
    for (k, s), ref in layout.got(values).items():
        place = layout.place(-k, s)
        begin = sum(sizes[:2]) if upper and k != layout.late[1] else 0
        rows_ref[pl.ds(place * whole, whole)] = ref[begin : begin + full].reshape(
            whole, depth, lanes
        )
        if half:
            at = pl.ds(pl.multiple_of(place * half, 8), half)
            halves_ref[at] = ref[begin + full : begin + full + half]
    across = lane_index(depth) % EY
    line = SIDE + 1
    copies, done = [], 0
    for c, first, count in middle_groups(layout, depth, upper):
        put = functools.partial(put_node, nodes_ref, depth)
        end = t_ref[ENDS + c]
        for i in range(first, first + count):
            for j in range(SIDE):
                row = c * INNER + SIDE * (i - 1) + j
                value = u_ref[row]
                if row - base < rows_ref.shape[0]:
                    value += rows_ref[row - base]
                else:
                    value += double(halves_ref, 2 * (row - base - rows_ref.shape[0]), depth)
                at = line * (done + i - first)
                put(at + j, value)
                if j == 0:
                    last = jnp.where(across == EY - 1, roll(end, EY - 1 - i), roll(value, -1))
                    put(at + SIDE, last)
        nodes = nodes_ref[pl.ds(line * done * depth, line * count * depth), :]
        part = pl.ds(line * done, line * count)
        slots_out_ref[part] = to_slots(nodes, select).reshape(line * count, depth, lanes)
        copy = pltpu.make_async_copy(
            slots_out_ref.at[part],
            out_ref.at[c, pl.ds(line * first, line * count)],
            sems.at[len(copies)],
        )
        copy.start()
        copies.append(copy)
        done += count
    return copies


def lower_kernel(layout, u_ref, t_ref, slots_ref, *refs):
    values, out_ref, scratch = refs[:-6], refs[-6], refs[-5:]
    select = pair_selector(slots_ref)
    for copy in middle_nodes(layout, False, u_ref, t_ref, select, values, out_ref, scratch):
        copy.wait()


def upper_kernel(layout, u_ref, t_ref, slots_ref, before_ref, after_ref, *refs):
    values, out_ref, scratch = refs[:-10], refs[-9], refs[-8:]
    select = pair_selector(slots_ref)
    copies = middle_nodes(layout, True, u_ref, t_ref, select, values, out_ref, scratch[:5])
    copies += faces_nodes(t_ref, before_ref, after_ref, select, out_ref, *scratch[5:])
    for copy in copies:
        copy.wait()


def middle_scratch(layout, depth, upper):
    sizes = layout.share(depth)
    groups = middle_groups(layout, depth, upper)
    count = (SIDE + 1) * sum(group[2] for group in groups)
    blocks = len(layout.blocks)
    full, half = sizes[2:] if upper else (sizes[0], 0)
    return [
        pltpu.VMEM((count * depth, 2 * LANES), bf16),
        pltpu.VMEM((count, depth, LANES), f32),
        pltpu.SemaphoreType.DMA((len(groups),)),
        pltpu.VMEM((blocks * full // depth, depth, LANES), f32),
        pltpu.VMEM((blocks * max(half, 8), LANES), f32),
    ]


def expand(kernel, name, scratch, args, result=None):
    depth = args[0].shape[1]
    in_specs = [pl.BlockSpec(memory_space=pltpu.VMEM)] * len(args)
    aliases = {}
    if result is not None:
        aliases = {len(args): 0}
        args = (*args, result)
        in_specs.append(pl.BlockSpec(memory_space=pl.ANY))
    return pl.pallas_call(
        kernel,
        in_specs=in_specs,
        out_specs=pl.BlockSpec(memory_space=pl.ANY),
        out_shape=jax.ShapeDtypeStruct((3, NODES, depth, LANES), f32),
        scratch_shapes=scratch,
        input_output_aliases=aliases,
        compiler_params=pltpu.CompilerParams(vmem_limit_bytes=VMEM),
        cost_estimate=pl.CostEstimate(flops=0, bytes_accessed=0, transcendentals=0),
        name=name,
    )(*args)


def beside(faces):
    count = lax.axis_size("dom")
    onward = [(k, (k + 1) % count) for k in range(count)]
    back = [(k, (k - 1) % count) for k in range(count)]
    before = lax.ppermute(faces, "dom", onward)
    return before, before if onward == back else lax.ppermute(faces, "dom", back)


def local(velocity, slot_of_cell, elem_mats, geometry):
    depth = velocity.shape[1]
    layout = Layout(lax.axis_size("modes"))
    args = (velocity.transpose(0, 2, 1, 3), slot_of_cell, elem_mats.transpose(1, 0, 2), geometry)
    table = jnp.asarray(operator(layout, depth))
    early, late = layout.start(*layout.divide(elements("mass", (3,), layout, args)))
    pencil = late + layout.middle(late) + layout.end(early)
    u, u_extras = elements("stiff", (0, 1, 2), None, args)
    table = following([table], u)[0]
    cut = sum(layout.share(depth)[:2])
    early, late = layout.start(*layout.divide(spanwise(layout, depth, pencil, table)))
    lower = layout.middle(late, slice(None, cut))
    upper = layout.middle(late, slice(cut, None))
    ended = layout.end(early)
    total, faces = totals(layout, u_extras, late + lower + ended)
    before, after = beside(faces)
    scratch = middle_scratch(layout, depth, False)
    args = (u, total, slot_of_cell)
    kernel = functools.partial(lower_kernel, layout)
    result = expand(kernel, "lower", scratch, (*args, *late, *lower, *ended))
    scratch = middle_scratch(layout, depth, True) + [
        pltpu.VMEM((2 * (SIDE + 1) * depth, 2 * LANES), bf16),
        pltpu.VMEM((3, 2, SIDE + 1, depth, LANES), f32),
        pltpu.SemaphoreType.DMA((3, 2)),
    ]
    kernel = functools.partial(upper_kernel, layout)
    args += (before, after, *late, *upper, *ended)
    result = expand(kernel, "upper", scratch, args, result)
    return result.transpose(0, 2, 1, 3)


def solution(mesh):
    in_specs = (P(None, "modes", None, "dom"), P("dom", None), P(), P(None, "dom"))
    out_specs = P(None, "modes", None, "dom")
    return jax.shard_map(local, mesh=mesh, in_specs=in_specs, out_specs=out_specs, check_vma=False)
```

```python
import functools
import math

import jax
import jax.numpy as jnp
import numpy as np
from jax import lax
from jax.experimental import pallas as pl
from jax.experimental.pallas import tpu as pltpu
from jax.sharding import PartitionSpec as P

EX = 16
EY = 8
LANES = EX * EY
NODES = 81
SIDE = 8
INNER = SIDE * (SIDE - 1)
FACE = SIDE * EY
HALF = LANES // 2
ENDS = 3 * SIDE
FACES = ENDS + 3
EXTRAS = FACES + 3
CORNERS = 2 * FACES + 3
HALVES = CORNERS + 1
DEEP = 96
PITCH = 104
TALL = 88
VMEM = 48 * 1024 * 1024
WIDE = 60 * 1024 * 1024

f32 = jnp.float32
bf16 = jnp.bfloat16


def split(values):
    high = values.astype(bf16)
    return high, (values - high.astype(f32)).astype(bf16)


class Layout:

    def __init__(self, parts):
        self.outer = max(d for d in range(1, math.isqrt(parts) + 1) if parts % d == 0)
        self.inner = parts // self.outer
        assert self.inner & (self.inner - 1) == 0
        self.late = [0, self.outer // 2]
        self.early = [k for k in range(1, self.outer) if k not in self.late]
        self.blocks = [(k, s) for k in range(self.outer) for s in range(self.inner)]

    def place(self, k, s):
        me = lax.axis_index("modes")
        out = lax.rem(me // self.inner + (k + self.outer), self.outer)
        return out * self.inner + jnp.bitwise_xor(lax.rem(me, self.inner), s)

    def sent(self, k, s, early, late):
        if k in self.late:
            return late[s].at[self.late.index(k)]
        return early[self.early.index(k)].at[s]

    def share(self, depth):
        count = len(self.blocks)
        full = 3 * INNER // count
        rest = -(-2 * (3 * INNER - full * count) // count)
        if rest == 2:
            full, rest = full + 1, 0
        lower = full // 2
        extra = -(-HALVES // count)
        return lower * depth, extra * depth // 2, (full - lower) * depth, rest * depth // 2

    def base(self, depth):
        return self.share(depth)[0] // depth * len(self.blocks)

    def shapes(self, share):
        early = [(self.inner,) + share] * len(self.early)
        return early + [(len(self.late),) + share] * self.inner

    def divide(self, arrays):
        return arrays[: len(self.early)], arrays[len(self.early) :]

    def got(self, refs):
        inner = self.inner
        late, middle, early = refs[:inner], refs[inner:], refs[inner + len(self.late) - 1 :]
        found = {(0, s): late[s].at[0] for s in range(inner)}
        for at, k in enumerate(self.late[1:]):
            found.update({(k, s): middle[at].at[s] for s in range(inner)})
        for at, k in enumerate(self.early):
            found.update({(k, s): early[s].at[at] for s in range(inner)})
        return found

    def onward(self, value, k):
        parts = self.outer * self.inner
        steps = [(d, (d + k * self.inner) % parts) for d in range(parts)]
        return lax.ppermute(value, "modes", steps)

    def across(self, values):
        pairs = lambda s: [(d, d ^ s) for d in range(self.outer * self.inner)]
        return values[:1] + [
            lax.ppermute(value, "modes", pairs(s)) for s, value in enumerate(values) if s
        ]

    def start(self, early, late):
        early = [self.onward(value, k) for k, value in zip(self.early, early)]
        return early, self.across(list(late))

    def middle(self, late, part=slice(None)):
        return [
            self.onward(jnp.stack([value[at, part] for value in late]), k)
            for at, k in enumerate(self.late)
            if k
        ]

    def end(self, early):
        return self.across([jnp.stack([value[s] for value in early]) for s in range(self.inner)])


def following(values, *earlier):
    return [lax.optimization_barrier((value, *earlier))[0] for value in values]


def operator(layout, depth):
    outer, inner = layout.outer, layout.inner
    length = outer * inner * depth
    half = length // 2
    waves = np.arange(half + 1)
    weights = np.where((waves == 0) | (waves == half), 1.0, 2.0) / length
    sigma = 1.0 + (8.0 * waves / length) ** 2
    phases = (np.arange(length)[:, None] * waves[None, :]) % length
    row = (np.cos(phases * (2.0 * np.pi / length)) * (weights * sigma)).sum(1)
    step, slot, plane = np.meshgrid(np.arange(outer), np.arange(inner), np.arange(depth), indexing="ij")
    step, slot, plane = step.ravel(), slot.ravel(), plane.ravel()
    place = np.arange(inner)[:, None]
    sent = (step * inner + (place ^ slot)) * depth + plane
    got = (-step * inner + (place ^ slot)) * depth + plane
    full = row[(sent[:, :, None] - got[:, None, :]) % length].astype(np.float32)
    high = full.astype(jnp.bfloat16)
    low = (full - high.astype(np.float32)).astype(jnp.bfloat16)
    return np.concatenate([high, low], axis=1)


def selector(slots):
    slot = lax.broadcasted_iota(jnp.int32, (LANES, LANES), 0)
    return jnp.where(slot == slots, 1.0, 0.0).astype(f32)


def lane_index(depth):
    return lax.broadcasted_iota(jnp.int32, (depth, LANES), 1)


def roll(value, shift):
    shift = shift % LANES
    return value if shift == 0 else pltpu.roll(value, shift, 1)


def gather_face(column, origin):
    lane = lane_index(column[0].shape[0])
    face = jnp.where(lane == FACE, roll(column[SIDE], FACE - origin - EY + 1), 0.0)
    for j in range(SIDE):
        face = jnp.where(lane // EY == j, roll(column[j], EY * j - origin), face)
    return face


def prepare(terms, slots_ref, mats_ref, left_ref):
    select = selector(slots_ref[...]).astype(bf16)
    left_ref[...] = jnp.zeros_like(left_ref)
    for place, term in enumerate(terms):
        high, low = split(mats_ref[:, term, :])
        left_ref[place, :NODES, 0:NODES] = high
        left_ref[place, :NODES, NODES : NODES + 1] = low[:, NODES - 1 :]
        left_ref[place, :NODES, TALL : TALL + NODES] = high
        left_ref[place, :NODES, 2 * TALL :] = low[:, : NODES - 1]
    return jnp.concatenate([select, select], axis=0)


def component(terms, first, second, select, geo, left, scratch, row, ends, face):
    values_ref, images_ref, cells_ref = scratch
    depth = first.shape[1]
    values_ref[:NODES, :depth] = first[...] * second[...]
    values_ref[NODES, :depth] = values_ref[NODES - 1, :depth]
    flat = values_ref.reshape((TALL + 1) * (depth + 8), LANES)
    for pair in range(0, depth, 2):
        right = []
        for p in (pair, pair + 1):
            value = flat[pl.ds(p, TALL, stride=depth + 8), :]
            high = value.astype(bf16).astype(f32)
            parts = jnp.concatenate([high, value - high, high[: NODES - 1]], axis=0)
            right.append(parts.astype(bf16))
        images = jnp.dot(left, jnp.concatenate(right, axis=1), preferred_element_type=f32)
        for p in (0, 1):
            total = 0.0
            for t, term in enumerate(terms):
                total = total + (
                    images[DEEP * t : DEEP * t + DEEP, LANES * p : LANES * p + LANES]
                    * geo[term : term + 1]
                )
            high, low = split(total)
            images_ref[(pair + p) * DEEP : (pair + p + 1) * DEEP, :LANES] = high
            images_ref[(pair + p) * DEEP : (pair + p + 1) * DEEP, LANES:] = low
    cells = jnp.dot(images_ref[...], select, preferred_element_type=f32)
    for p in range(depth):
        cells_ref[p * PITCH : p * PITCH + DEEP] = cells[p * DEEP : (p + 1) * DEEP]
    lane = lane_index(depth)
    across = lane % EY

    def node(i, j):
        value = cells_ref[pl.ds((SIDE + 1) * i + j, depth, stride=PITCH), :]
        if i > 0:
            return value
        return value + jnp.where(lane >= EY, roll(node(8, j), EY), 0.0)

    def join(low, high):
        return low + jnp.where(across > 0, roll(high, 1), 0.0)

    end = jnp.zeros((depth, LANES), f32)
    for i in range(SIDE + 1):
        column = [node(i, j) for j in range(SIDE + 1)]
        column[0] = join(column[0], column[SIDE])
        if i < SIDE:
            for j in range(SIDE):
                row(SIDE * (i - 1) + j if i else INNER + j, column[j])
            end = jnp.where(across == i, roll(column[SIDE], i + 1 - EY), end)
    ends(end)
    face(gather_face(column, LANES - EY))


def pack(value, half):
    lane = lane_index(value.shape[0] // 2)
    top, bottom = value[: value.shape[0] // 2], value[value.shape[0] // 2 :]
    if half:
        return jnp.where(lane < HALF, roll(top, HALF), bottom)
    return jnp.where(lane < HALF, top, roll(bottom, HALF))


def unpack(packed):
    return jnp.concatenate([packed, roll(packed, HALF)], axis=0)


def element_kernel(terms, layout, count, *refs):
    vel_hbm, slots_hbm, mats_hbm, geo_hbm = refs[:4]
    outs, scratch = refs[4 : 4 + count], refs[4 + count :]
    vel_ref, slots_ref, mats_ref, geo_ref, left_ref, *parts, sems = scratch[:9]
    pairs = [(slots_hbm, slots_ref), (geo_hbm, geo_ref), (mats_hbm, mats_ref)]
    pairs += [(vel_hbm.at[c], vel_ref.at[c]) for c in range(3)]
    copies = [pltpu.make_async_copy(*pair, sems.at[k]) for k, pair in enumerate(pairs)]
    for k in (3, 2, 4, 0, 1, 5):
        copies[k].start()
    depth = vel_ref.shape[2]
    parts[0][NODES:] = jnp.zeros((TALL + 1 - NODES, depth + 8, LANES), f32)
    sends = []
    corners = [jnp.zeros((depth, LANES), f32)]
    if layout:
        blocks_ref, send_sems = scratch[9:]
        early, late = layout.divide(outs)
        sizes, base = layout.share(depth), layout.base(depth)
        total, lower = sum(sizes), sizes[0]
        full = base + sizes[2] // depth * len(layout.blocks)
        for k, s in layout.blocks:
            place, target = layout.place(k, s), layout.sent(k, s, early, late)
            for begin, end in ((0, lower), (lower, total)):
                source = pl.ds(pl.multiple_of(place * total + begin, 8), end - begin)
                copy = pltpu.make_async_copy(
                    blocks_ref.at[source], target.at[begin:end], send_sems.at[len(sends)]
                )
                sends.append((place, copy))

    def put_block(kind, at, value):
        size = value.shape[0]
        count = sizes[kind] // size
        begin = at // count * total + sum(sizes[:kind]) + at % count * size
        blocks_ref[begin : begin + size] = value

    def put_half(kind, at, value, half=0):
        put_block(kind, at, pack(value, half))

    def put_extra(row, value):
        if layout:
            put_half(1, 2 * row, value)
            put_half(1, 2 * row + 1, value, 1)
        else:
            outs[1][row] = value

    def put_row(c, row, value):
        if row >= INNER:
            put_extra(SIDE * c + row - INNER, value)
            return
        row += c * INNER
        if not layout:
            outs[0][row] = value
        elif row < base:
            put_block(0, row, value)
        elif row < full:
            put_block(2, row - base, value)
        else:
            put_half(3, 2 * (row - full), value)
            put_half(3, 2 * (row - full) + 1, value, 1)

    def put_end(c, value):
        put_extra(ENDS + c, value)

    def put_face(c, value):
        if layout:
            put_half(1, 2 * FACES + c, value)
            corners[0] = jnp.where(lane_index(depth) == c, roll(value, c - FACE), corners[0])
        else:
            outs[1][FACES + c] = value

    for copy in copies[:3]:
        copy.wait()
    select = prepare(terms, slots_ref, mats_ref, left_ref)
    left = left_ref[...].reshape(len(terms) * DEEP, 2 * LANES)
    geo = geo_ref[...]
    copies[3].wait()
    for c in range(3):
        if c < 2:
            copies[4 + c].wait()
        puts = [functools.partial(store, c) for store in (put_row, put_end, put_face)]
        first, second = vel_ref.at[c], vel_ref.at[(c + 1) % 3]
        component(terms, first, second, select, geo, left, parts, *puts)
        for place, copy in sends[::2]:
            count = lower // depth
            before, ready = (min(len(layout.blocks), k * INNER // count) for k in (c, c + 1))
            if before < ready:
                pl.when(jnp.logical_and(place >= before, place < ready))(copy.start)
    if layout:
        put_half(1, CORNERS, corners[0])
        blank = jnp.zeros((depth, LANES), f32)
        for at in range(HALVES, sizes[1] * 2 // depth * len(layout.blocks)):
            put_half(1, at, blank)
        for at in range(3 * INNER - base, full - base):
            put_block(2, at, blank)
        for at in range(2 * max(3 * INNER - full, 0), sizes[3] * 2 // depth * len(layout.blocks)):
            put_half(3, at, blank)
        for _, copy in sends[1::2]:
            copy.start()
        for _, copy in sends:
            copy.wait()


def elements(name, terms, layout, args):
    depth = args[0].shape[2]
    scratch = [
        *(pltpu.VMEM(a.shape, a.dtype) for a in args),
        pltpu.VMEM((len(terms), DEEP, 2 * LANES), bf16),
        pltpu.VMEM((TALL + 1, depth + 8, LANES), f32),
        pltpu.VMEM((DEEP * depth, 2 * LANES), bf16),
        pltpu.VMEM((PITCH * (depth + 1), LANES), f32),
        pltpu.SemaphoreType.DMA((6,)),
    ]
    anywhere, vmem = pl.BlockSpec(memory_space=pl.ANY), pl.BlockSpec(memory_space=pltpu.VMEM)
    shapes, specs = [(3 * INNER, depth, LANES)], [vmem]
    if layout:
        count = len(layout.blocks)
        sizes = layout.share(depth)
        scratch.append(pltpu.VMEM((count * sum(sizes), LANES), f32))
        scratch.append(pltpu.SemaphoreType.DMA((2 * count,)))
        shapes = layout.shapes((sum(sizes), LANES))
        specs = [anywhere] * len(shapes)
    else:
        shapes.append((EXTRAS, depth, LANES))
        specs.append(vmem)
    return pl.pallas_call(
        functools.partial(element_kernel, terms, layout, len(shapes)),
        in_specs=[anywhere] * len(args),
        out_specs=specs,
        out_shape=[jax.ShapeDtypeStruct(shape, f32) for shape in shapes],
        scratch_shapes=scratch,
        compiler_params=pltpu.CompilerParams(vmem_limit_bytes=WIDE if layout else VMEM),
        cost_estimate=pl.CostEstimate(
            flops=2 * 3 * depth * len(terms) * DEEP * 3 * DEEP * LANES,
            bytes_accessed=4 * 3 * depth * LANES * 150,
            transcendentals=0,
        ),
        name=name,
    )(*args)


def left_sums(before, j):
    lane = lane_index(before.shape[0])
    if j < SIDE:
        return jnp.where(lane < EY, roll(before, -EY * j), 0.0)
    return jnp.where(lane == 0, roll(before, -FACE), 0.0)


def spanwise_kernel(layout, depth, count, *refs):
    got = layout.got(refs[:count])
    table_ref, early, late = refs[count], *layout.divide(refs[count + 1 :])
    length = len(layout.blocks) * depth
    table = table_ref[lax.rem(lax.axis_index("modes"), layout.inner)]
    rows, begin = [], 0
    for sublanes, size in zip(layout.share(depth), (depth, depth // 2) * 2):
        rows += [(at, size) for at in range(begin, begin + sublanes, size)]
        begin += sublanes
    for first in range(0, len(rows), 2):
        group = rows[first : first + 2]
        x = []
        for at, size in group:
            blocks = [got[block][at : at + size] for block in layout.blocks]
            if size < depth:
                blocks = [unpack(block) for block in blocks]
            x.append(jnp.concatenate(blocks, axis=0))
        x_high, x_low = split(jnp.concatenate(x, axis=1))
        y = jnp.dot(table, x_high, preferred_element_type=f32)
        y = y[:length] + y[length:]
        y += jnp.dot(table[:length], x_low, preferred_element_type=f32)
        for place, block in enumerate(layout.blocks):
            for k, (at, size) in enumerate(group):
                value = y[depth * place : depth * place + depth, LANES * k : LANES * k + LANES]
                value = value if size == depth else pack(value, 0)
                layout.sent(*block, early, late)[at : at + size] = value


def spanwise(layout, depth, values, table):
    length = len(layout.blocks) * depth
    sizes = layout.share(depth)
    shapes = layout.shapes((sum(sizes), LANES))
    return pl.pallas_call(
        functools.partial(spanwise_kernel, layout, depth, len(values)),
        out_shape=[jax.ShapeDtypeStruct(shape, f32) for shape in shapes],
        compiler_params=pltpu.CompilerParams(vmem_limit_bytes=VMEM),
        cost_estimate=pl.CostEstimate(
            flops=6 * length * len(layout.blocks) * sum(sizes) * LANES,
            bytes_accessed=8 * len(layout.blocks) * sum(sizes) * LANES,
            transcendentals=0,
        ),
        name="spanwise",
    )(*values, table)


def to_slots(nodes, select):
    return lax.dot_general(nodes, select, (((1,), (1,)), ((), ())), preferred_element_type=f32)


def pair_selector(slots_ref):
    select = selector(slots_ref[...]).astype(bf16)
    return jnp.concatenate([select, select], axis=1)


def single(ref, at, depth):
    return unpack(ref[at * depth // 2 : (at + 1) * depth // 2])


def double(ref, at, depth):
    lower, upper = single(ref, at, depth), single(ref, at + 1, depth)
    return jnp.where(lane_index(depth) < HALF, lower, roll(upper, HALF))


def totals_kernel(layout, u_ref, *refs):
    total_ref, faces_ref, halves_ref = refs[-3:]
    depth = u_ref.shape[1]
    begin, size = layout.share(depth)[:2]
    for (k, s), ref in layout.got(refs[:-3]).items():
        at = pl.ds(pl.multiple_of(layout.place(-k, s) * size, 8), size)
        halves_ref[at] = ref[begin : begin + size]
    corners = single(halves_ref, CORNERS, depth)
    lane = lane_index(depth)
    last = jnp.zeros((depth, LANES), f32)
    for c in range(3):
        column = []
        for j in range(SIDE + 1):
            row = ENDS + c if j == SIDE else SIDE * c + j
            column.append(u_ref[row] + double(halves_ref, 2 * row, depth))
            total_ref[row] = column[j]
        face = single(halves_ref, 2 * FACES + c, depth)
        face = jnp.where(lane_index(depth) == FACE, roll(corners, FACE - c), face)
        face += u_ref[FACES + c]
        total_ref[FACES + c] = face
        left = gather_face(column[:SIDE] + [roll(column[SIDE], EY - 1)], 0)
        faces_ref[c] = jnp.where(lane < HALF, face, roll(left, HALF))
        last = jnp.where(lane == c, roll(face, c - FACE), last)
        last = jnp.where(lane == SIDE + c, roll(left, SIDE + c - FACE), last)
    faces_ref[3] = last


def totals(layout, u, values):
    depth = u.shape[1]
    size = layout.share(depth)[1]
    return pl.pallas_call(
        functools.partial(totals_kernel, layout),
        out_shape=[
            jax.ShapeDtypeStruct(u.shape, f32),
            jax.ShapeDtypeStruct((4, depth, LANES), f32),
        ],
        scratch_shapes=[pltpu.VMEM((len(layout.blocks) * size, LANES), f32)],
        compiler_params=pltpu.CompilerParams(vmem_limit_bytes=VMEM),
        cost_estimate=pl.CostEstimate(flops=0, bytes_accessed=0, transcendentals=0),
        name="totals",
    )(u, *values)


def put_node(nodes_ref, depth, at, value):
    high, low = split(value)
    nodes_ref[pl.ds(at * depth, depth), :] = jnp.concatenate([high, low], axis=1)


def faces_nodes(t_ref, before_ref, after_ref, select, out_ref, nodes_ref, slots_out_ref, sems):
    depth, lanes = t_ref.shape[1:]
    lane = lane_index(depth)
    across = lane % EY
    count = SIDE + 1
    copies = []
    for c in range(3):
        put = functools.partial(put_node, nodes_ref, depth)
        before = jnp.where(lane == FACE, roll(before_ref[3], FACE - c), before_ref[c])
        after = roll(after_ref[c], HALF)
        after = jnp.where(lane == FACE, roll(after_ref[3], FACE - SIDE - c), after)
        face = t_ref[FACES + c] + after
        end = t_ref[ENDS + c] + left_sums(before, SIDE)
        for j in range(SIDE):
            value = t_ref[SIDE * c + j] + left_sums(before, j)
            moved = roll(face, lanes - EY - EY * j)
            beyond = jnp.where(lane >= lanes - EY, moved, roll(value, -EY))
            put(j, value)
            put(count + j, beyond)
            if j == 0:
                last = jnp.where(across == EY - 1, roll(end, EY - 1), roll(value, -1))
                put(SIDE, last)
                corner = jnp.where(across == EY - 1, roll(end, -1), roll(beyond, -1))
                corner = jnp.where(lane == lanes - 1, roll(face, lanes - 1 - FACE), corner)
                put(count + SIDE, corner)
        slots_out_ref[c] = to_slots(nodes_ref[...], select).reshape(2, count, depth, lanes)
        for side in range(2):
            copy = pltpu.make_async_copy(
                slots_out_ref.at[c, side],
                out_ref.at[c, pl.ds(side * (NODES - count), count)],
                sems.at[c, side],
            )
            copy.start()
            copies.append(copy)
    return copies


def middle_groups(layout, depth, upper):
    group = SIDE - 1
    cut = layout.base(depth) // SIDE
    first, last = (cut, 3 * group) if upper else (0, cut)
    groups = []
    while first < last:
        count = min(last - first, group - first % group)
        groups.append((first // group, first % group + 1, count))
        first += count
    return groups


def middle_nodes(layout, upper, u_ref, t_ref, select, values, out_ref, scratch):
    nodes_ref, slots_out_ref, sems, rows_ref, halves_ref = scratch
    depth, lanes = u_ref.shape[1:]
    sizes = layout.share(depth)
    full, half = sizes[2:] if upper else (sizes[0], 0)
    base = layout.base(depth) if upper else 0
    whole = full // depth
    for (k, s), ref in layout.got(values).items():
        place = layout.place(-k, s)
        begin = sum(sizes[:2]) if upper and k != layout.late[1] else 0
        rows_ref[pl.ds(place * whole, whole)] = ref[begin : begin + full].reshape(
            whole, depth, lanes
        )
        if half:
            at = pl.ds(pl.multiple_of(place * half, 8), half)
            halves_ref[at] = ref[begin + full : begin + full + half]
    across = lane_index(depth) % EY
    line = SIDE + 1
    copies, done = [], 0
    for c, first, count in middle_groups(layout, depth, upper):
        put = functools.partial(put_node, nodes_ref, depth)
        end = t_ref[ENDS + c]
        for i in range(first, first + count):
            for j in range(SIDE):
                row = c * INNER + SIDE * (i - 1) + j
                value = u_ref[row]
                if row - base < rows_ref.shape[0]:
                    value += rows_ref[row - base]
                else:
                    value += double(halves_ref, 2 * (row - base - rows_ref.shape[0]), depth)
                at = line * (done + i - first)
                put(at + j, value)
                if j == 0:
                    last = jnp.where(across == EY - 1, roll(end, EY - 1 - i), roll(value, -1))
                    put(at + SIDE, last)
        nodes = nodes_ref[pl.ds(line * done * depth, line * count * depth), :]
        part = pl.ds(line * done, line * count)
        slots_out_ref[part] = to_slots(nodes, select).reshape(line * count, depth, lanes)
        copy = pltpu.make_async_copy(
            slots_out_ref.at[part],
            out_ref.at[c, pl.ds(line * first, line * count)],
            sems.at[len(copies)],
        )
        copy.start()
        copies.append(copy)
        done += count
    return copies


def lower_kernel(layout, u_ref, t_ref, slots_ref, *refs):
    values, out_ref, scratch = refs[:-6], refs[-6], refs[-5:]
    select = pair_selector(slots_ref)
    for copy in middle_nodes(layout, False, u_ref, t_ref, select, values, out_ref, scratch):
        copy.wait()


def upper_kernel(layout, u_ref, t_ref, slots_ref, before_ref, after_ref, *refs):
    values, out_ref, scratch = refs[:-10], refs[-9], refs[-8:]
    select = pair_selector(slots_ref)
    copies = middle_nodes(layout, True, u_ref, t_ref, select, values, out_ref, scratch[:5])
    copies += faces_nodes(t_ref, before_ref, after_ref, select, out_ref, *scratch[5:])
    for copy in copies:
        copy.wait()


def middle_scratch(layout, depth, upper):
    sizes = layout.share(depth)
    groups = middle_groups(layout, depth, upper)
    count = (SIDE + 1) * sum(group[2] for group in groups)
    blocks = len(layout.blocks)
    full, half = sizes[2:] if upper else (sizes[0], 0)
    return [
        pltpu.VMEM((count * depth, 2 * LANES), bf16),
        pltpu.VMEM((count, depth, LANES), f32),
        pltpu.SemaphoreType.DMA((len(groups),)),
        pltpu.VMEM((blocks * full // depth, depth, LANES), f32),
        pltpu.VMEM((blocks * max(half, 8), LANES), f32),
    ]


def expand(kernel, name, scratch, args, result=None):
    depth = args[0].shape[1]
    in_specs = [pl.BlockSpec(memory_space=pltpu.VMEM)] * len(args)
    aliases = {}
    if result is not None:
        aliases = {len(args): 0}
        args = (*args, result)
        in_specs.append(pl.BlockSpec(memory_space=pl.ANY))
    return pl.pallas_call(
        kernel,
        in_specs=in_specs,
        out_specs=pl.BlockSpec(memory_space=pl.ANY),
        out_shape=jax.ShapeDtypeStruct((3, NODES, depth, LANES), f32),
        scratch_shapes=scratch,
        input_output_aliases=aliases,
        compiler_params=pltpu.CompilerParams(vmem_limit_bytes=VMEM),
        cost_estimate=pl.CostEstimate(flops=0, bytes_accessed=0, transcendentals=0),
        name=name,
    )(*args)


def beside(faces):
    count = lax.axis_size("dom")
    onward = [(k, (k + 1) % count) for k in range(count)]
    back = [(k, (k - 1) % count) for k in range(count)]
    before = lax.ppermute(faces, "dom", onward)
    return before, before if onward == back else lax.ppermute(faces, "dom", back)


def local(velocity, slot_of_cell, elem_mats, geometry):
    depth = velocity.shape[1]
    layout = Layout(lax.axis_size("modes"))
    args = (velocity.transpose(0, 2, 1, 3), slot_of_cell, elem_mats.transpose(1, 0, 2), geometry)
    table = jnp.asarray(operator(layout, depth))
    early, late = layout.start(*layout.divide(elements("mass", (3,), layout, args)))
    pencil = late + layout.middle(late) + layout.end(early)
    u, u_extras = elements("stiff", (0, 1, 2), None, args)
    table = following([table], u)[0]
    cut = sum(layout.share(depth)[:2])
    early, late = layout.start(*layout.divide(spanwise(layout, depth, pencil, table)))
    lower = layout.middle(late, slice(None, cut))
    upper = layout.middle(late, slice(cut, None))
    ended = layout.end(early)
    total, faces = totals(layout, u_extras, late + lower + ended)
    before, after = beside(faces)
    scratch = middle_scratch(layout, depth, False)
    args = (u, total, slot_of_cell)
    kernel = functools.partial(lower_kernel, layout)
    result = expand(kernel, "lower", scratch, (*args, *late, *lower, *ended))
    scratch = middle_scratch(layout, depth, True) + [
        pltpu.VMEM((2 * (SIDE + 1) * depth, 2 * LANES), bf16),
        pltpu.VMEM((3, 2, SIDE + 1, depth, LANES), f32),
        pltpu.SemaphoreType.DMA((3, 2)),
    ]
    kernel = functools.partial(upper_kernel, layout)
    args += (before, after, *late, *upper, *ended)
    result = expand(kernel, "upper", scratch, args, result)
    return result.transpose(0, 2, 1, 3)


def solution(mesh):
    in_specs = (P(None, "modes", None, "dom"), P("dom", None), P(), P(None, "dom"))
    out_specs = P(None, "modes", None, "dom")
    return jax.shard_map(local, mesh=mesh, in_specs=in_specs, out_specs=out_specs, check_vma=False)
```
